256 devices in a mesh: tm: 16 (over x, y), rows: 16 (over z, core).
Axes of the slice: x: 4, y: 4, z: 8, core: 2. Of those that a mesh axis runs over, the one named last changes fastest.
Arguments:
- latents: bfloat16 [128, 64, 64, 256], P('tm', 'rows'), may hold values from -6 to 6
- cotangent: bfloat16 [128, 64, 64, 256], P('tm', 'rows'), may hold values from -6 to 6
- w_spatial: bfloat16 [9, 256, 256], replicated, may hold values from -0.125 to 0.125
- w_time: bfloat16 [4, 2, 256, 256], replicated, may hold values from -0.25 to 0.25
Outputs:
- block_out: bfloat16 [128, 64, 64, 256], P('tm', 'rows')
- input_grad: bfloat16 [128, 64, 64, 256], P('tm', 'rows')
- spatial_grad: float32 [9, 256, 256], P(None, None, 'rows')
- time_grad: float32 [4, 2, 256, 256], P(None, None, None, 'rows')
The draws below stay inside these ranges and needn't reach their ends.
All inputs are finite; a program needn't handle non-finite values.
Results may differ from the reference program's by a relative error of at most 0.013.
Values may be sent and summed in bfloat16 or wider, within the bound.
A program may use at most 128 MiB of HBM per device.

```python
import math
import jax
import jax.numpy as jnp

C = 256
WIDTH = 64
FRAMES = 128
HEIGHT = 64


def level_of(key, extent, pieces, smallest, largest):
    gain = 1.0
    for dim, parts in pieces:
        heights = jax.random.uniform(jax.random.fold_in(jax.random.fold_in(key, 6), dim), (parts,), jnp.float32, smallest / len(pieces), largest / len(pieces))
        gain = gain * jnp.repeat(jnp.exp(heights), extent[dim] // parts).reshape((-1,) + (1,) * (len(extent) - 1 - dim))
    return gain


def normal_values(rng, shape, scale, reach, split=(), held_as=jnp.bfloat16):
    level = level_of(rng, shape, split, -0.22, 0.18) if split else 1.0
    entries = jax.random.normal(rng, shape, jnp.float32) * scale * level
    return jnp.minimum(jnp.maximum(entries, -reach), reach).astype(held_as)


def setup_inputs(seed: int = 0) -> dict:
    key_of = jax.random.split(jax.random.key(seed), 5)
    latents = normal_values(key_of[0], (FRAMES, HEIGHT, WIDTH, C), 1.0, 6.0, ((0, 16), (1, 16)))
    cotangent = normal_values(key_of[1], (FRAMES, HEIGHT, WIDTH, C), 1.0, 6.0, ((0, 16), (1, 16)))
    w_spatial = normal_values(key_of[2], (9, C, C), (9 * C) ** -0.5, 0.125)
    w_time = normal_values(key_of[3], (4, 2, C, C), (2 * C) ** -0.5, 0.25)
    return dict(latents=latents, cotangent=cotangent, w_spatial=w_spatial, w_time=w_time)


def project(values, weight):
    flat = values.reshape(-1, values.shape[-1])
    return jnp.dot(flat, weight, preferred_element_type=jnp.float32).reshape(values.shape[:-1] + (weight.shape[-1],))

def contract_rows(left, right):
    left_flat = left.reshape(-1, left.shape[-1])
    right_flat = right.reshape(-1, right.shape[-1])
    return jnp.dot(left_flat.T, right_flat, preferred_element_type=jnp.float32)

def delay_frames(values, dilation):
    return jnp.concatenate([jnp.zeros_like(values[:dilation]), values[:-dilation]], axis=0)

def advance_frames(values, dilation):
    return jnp.concatenate([values[dilation:], jnp.zeros_like(values[:dilation])], axis=0)

def silu_slope(values):
    sigma = jax.nn.sigmoid(values)
    return sigma * (1.0 + values * (1.0 - sigma))

def reference(latents, cotangent, w_spatial, w_time):
    height = latents.shape[1]
    width = latents.shape[2]
    padded = jnp.pad(latents, ((0, 0), (1, 1), (1, 1), (0, 0)))
    preact = jnp.zeros(latents.shape, jnp.float32)
    for shift_row in range(3):
        for shift_col in range(3):
            window = padded[:, shift_row:shift_row + height, shift_col:shift_col + width]
            preact = preact + project(window, w_spatial[3 * shift_row + shift_col])
    state = jax.nn.silu(preact).astype(jnp.bfloat16)
    states = []
    temporals = []
    for layer in range(4):
        dilation = 2 ** layer
        states.append(state)
        temporal = project(state, w_time[layer, 0]) + project(delay_frames(state, dilation), w_time[layer, 1])
        temporals.append(temporal)
        if layer < 3:
            state = jax.nn.silu(temporal).astype(jnp.bfloat16)
    block_out = (latents.astype(jnp.float32) + temporal).astype(jnp.bfloat16)
    factor = 1.0 / math.sqrt(FRAMES * HEIGHT * WIDTH)
    delta = cotangent
    time_parts = [None] * 4
    for layer in range(3, -1, -1):
        dilation = 2 ** layer
        grad_now = contract_rows(states[layer], delta)
        grad_past = contract_rows(delay_frames(states[layer], dilation), delta)
        time_parts[layer] = jnp.stack([grad_now, grad_past]) * factor
        back = project(delta, w_time[layer, 0].T) + project(advance_frames(delta, dilation), w_time[layer, 1].T)
        if layer > 0:
            delta = (back * silu_slope(temporals[layer - 1])).astype(jnp.bfloat16)
        else:
            spatial_delta = (back * silu_slope(preact)).astype(jnp.bfloat16)
    time_grad = jnp.stack(time_parts)
    padded_delta = jnp.pad(spatial_delta, ((0, 0), (1, 1), (1, 1), (0, 0)))
    input_grad = cotangent.astype(jnp.float32)
    spatial_parts = []
    for shift_row in range(3):
        for shift_col in range(3):
            kernel = w_spatial[3 * shift_row + shift_col]
            window = padded[:, shift_row:shift_row + height, shift_col:shift_col + width]
            spatial_parts.append(contract_rows(window, spatial_delta) * factor)
            source = padded_delta[:, 2 - shift_row:2 - shift_row + height, 2 - shift_col:2 - shift_col + width]
            input_grad = input_grad + project(source, kernel.T)
    spatial_grad = jnp.stack(spatial_parts)
    return (block_out, input_grad.astype(jnp.bfloat16), spatial_grad, time_grad)
```

```python
import math

import jax
import jax.numpy as jnp
from jax import lax
from jax.experimental import pallas as pl
from jax.experimental.pallas import tpu as pltpu
from jax.sharding import PartitionSpec as P

MESH = pl.DeviceIdType.MESH
F = 8
N = 256
BF = jnp.bfloat16
F32 = jnp.float32


def dot(a, b):
    return lax.dot_general(a, b, (((1,), (0,)), ((), ())), preferred_element_type=F32)


def columns(v):
    wide = v.astype(F32)
    n = wide.shape[0]
    col = lax.rem(lax.broadcasted_iota(jnp.int32, wide.shape, 0), 64)
    left = jnp.where(col == 0, 0.0, pltpu.roll(wide, 1, 0)).astype(BF)
    right = jnp.where(col == 63, 0.0, pltpu.roll(wide, n - 1, 0)).astype(BF)
    return left, right


def kernel(
    lat, cot, ws, wt,
    out, gin, gs_out, gt_out,
    xs, ys, lat_lo, lat_hi, sd_lo, sd_hi,
    s0, s1, s2, s3, slope, d0, d1, d2, d3h, sd, dT, wsT, wtT,
    g_t, g_s, ra_t, ra_s, ma_t, ma_s, rb_t, rb_s, mb_t, mb_s, rc_t, rc_s, mc_t, mc_s,
    row_sem, tm_sem, a_sem, b_send, b_recv, c_send, c_recv, h_send, h_recv,
):
    t = lax.axis_index("tm")
    r = lax.axis_index("rows")
    z = r // 2
    c = lax.rem(r, 2)
    tm_next = lax.rem(t + 1, 16)
    tm_prev = lax.rem(t + 15, 16)
    r_next = lax.rem(r + 1, 16)
    r_prev = lax.rem(r + 15, 16)
    sibling = r + 1 - 2 * c
    far = lax.rem(r + 15 + 2 * c, 16)
    states = (s0, s1, s2, s3)
    deltas = (d0, d1, d2)
    factor = 1.0 / math.sqrt(524288.0)

    barrier = pltpu.get_barrier_semaphore()
    for k in range(1, 16):
        pl.semaphore_signal(barrier, inc=1, device_id=(lax.rem(t + k, 16), r), device_id_type=MESH)
    for k in range(1, 8):
        pl.semaphore_signal(
            barrier, inc=1, device_id=(t, lax.rem(r + 2 * k, 16)), device_id_type=MESH
        )
    pl.semaphore_signal(barrier, inc=1, device_id=(t, sibling), device_id_type=MESH)
    pl.semaphore_signal(barrier, inc=1, device_id=(t, far), device_id_type=MESH)
    pl.semaphore_wait(barrier, 24)

    def remote(src, dst, send, recv, device):
        return pltpu.make_async_remote_copy(
            src_ref=src, dst_ref=dst, send_sem=send, recv_sem=recv, device_id=device,
            device_id_type=MESH,
        )

    lat_up = remote(lat.at[:, 192:256], lat_lo, row_sem.at[0], row_sem.at[1], (t, r_next))
    lat_dn = remote(lat.at[:, 0:64], lat_hi, row_sem.at[2], row_sem.at[3], (t, r_prev))
    lat_up.start()
    lat_dn.start()
    cot_dn = remote(cot, d3h, tm_sem.at[0], tm_sem.at[1], (tm_prev, r))
    cot_dn.start()
    state_up = [
        remote(
            states[k].at[8 : 8 + 2**k], states[k].at[0 : 2**k],
            tm_sem.at[2 + 2 * k], tm_sem.at[3 + 2 * k], (tm_next, r),
        )
        for k in range(4)
    ]
    delta_dn = [
        remote(
            deltas[k].at[0 : 2**k], deltas[k].at[8 : 8 + 2**k],
            tm_sem.at[10 + 2 * k], tm_sem.at[11 + 2 * k], (tm_prev, r),
        )
        for k in range(3)
    ]

    @pl.loop(0, F)
    def _(f):
        v = lat[f]
        left, right = columns(v)
        xs[f, 64:320, 0:256] = left
        xs[f, 64:320, 256:512] = v
        xs[f, 64:320, 512:768] = right

    for i in range(3):
        for j in range(3):
            wsT[i, 256 * j : 256 * j + 256, :] = ws[i, 256 * j : 256 * j + 256, :].T

    @pl.loop(0, 4)
    def _(k):
        wtT[k, 0:256, :] = wt[k, 0:256, :].T
        wtT[k, 256:512, :] = wt[k, 256:512, :].T

    lat_up.wait()
    lat_dn.wait()

    @pl.when(r == 0)
    def _():
        lat_lo[...] = jnp.zeros_like(lat_lo)

    @pl.when(r == 15)
    def _():
        lat_hi[...] = jnp.zeros_like(lat_hi)

    @pl.loop(0, F)
    def _(f):
        for ref, at in ((lat_lo, 0), (lat_hi, 320)):
            v = ref[f]
            left, right = columns(v)
            xs[f, at : at + 64, 0:256] = left
            xs[f, at : at + 64, 256:512] = v
            xs[f, at : at + 64, 512:768] = right

    def activate(k, f, n, v):
        sigma = 0.5 + 0.5 * jnp.tanh(0.5 * v)
        state = v * sigma
        states[k][pl.ds(2**k + f, n)] = state.astype(BF).reshape(n, N, N)
        slope[k, pl.ds(f, n)] = (sigma + state * (1.0 - sigma)).reshape(n, N, N)

    def blocks(low, high, body):
        f = low
        if (high - low) >= 4 and (high - low) % 2 == 0:
            @pl.loop(low // 2 * 2, high, step=2)
            def _(g):
                body(g, 2)
            return
        while f < high:
            n = min(2, high - f)
            body(f, n)
            f += n

    @pl.loop(0, F // 2)
    def _(b):
        f = 2 * b
        cat = jnp.concatenate(
            [xs[pl.ds(f, 2), 64 * i : 64 * i + 256, :].reshape(512, 768) for i in range(3)], axis=1
        )
        activate(0, f, 2, dot(cat, ws[...].reshape(2304, 256)))

    state_up[0].start()

    def past(ref, at, n):
        return ref[pl.ds(at, n)].reshape(n * N, N)

    def temporal(k, f, n):
        cat = jnp.concatenate(
            [past(states[k], f + 2**k, n), past(states[k], f, n)], axis=1
        )
        return dot(cat, wt[k])

    def forward(k):
        def body(f, n):
            activate(k + 1, f, n, temporal(k, f, n))
        return body

    def arrived_state(k):
        state_up[k].wait()

        @pl.when(t == 0)
        def _():
            states[k][0 : 2**k] = jnp.zeros((2**k, N, N), BF)

    f0 = forward(0)
    blocks(2, 8, f0)
    state_up[1].start()
    f0(1, 1)
    f1 = forward(1)
    blocks(4, 8, f1)
    state_up[2].start()
    f1(3, 1)
    arrived_state(0)
    f0(0, 1)
    arrived_state(1)
    f1(0, 2)
    f1(2, 1)
    f2 = forward(2)
    blocks(4, 8, f2)
    arrived_state(2)
    blocks(0, 4, f2)
    state_up[3].start()

    def delta_of(k):
        def body(f, n):
            if k == 3:
                now, later = past(cot, f, n), past(d3h, f, n)
            else:
                now, later = past(deltas[k], f, n), past(deltas[k], f + 2**k, n)
            back = dot(jnp.concatenate([now, later], axis=1), wtT[k])
            value = (back * slope[k, pl.ds(f, n)].reshape(n * N, N)).astype(BF)
            target = sd if k == 0 else deltas[k - 1]
            target[pl.ds(f, n)] = value.reshape(n, N, N)
        return body

    def put(ref, tap, value):
        for part in range(16):
            ref[part % 2, part // 2, tap] = value[16 * part : 16 * part + 16].astype(BF)

    def time_grads(k):
        d = 2**k
        for f in range(F):
            src = cot if k == 3 else deltas[k]
            dT[0:256, 256 * f : 256 * f + 256] = src[f].T
            other = d3h[f] if k == 3 else deltas[k][f + d]
            dT[256:512, 256 * f : 256 * f + 256] = other.T
        both = dot(dT[...], states[k][d : d + F].reshape(2048, N))
        put(g_t, 2 * k, both[0:256])
        put(g_t, 2 * k + 1, both[256:512])

    def arrived_delta(k):
        copy = cot_dn if k == 3 else delta_dn[k]
        copy.wait()

        @pl.when(t == 15)
        def _():
            if k == 3:
                d3h[...] = jnp.zeros_like(d3h)
            else:
                deltas[k][8 : 8 + 2**k] = jnp.zeros((2**k, N, N), BF)

    b3, b2, b1, b0 = delta_of(3), delta_of(2), delta_of(1), delta_of(0)
    arrived_delta(3)
    blocks(0, 4, b3)
    delta_dn[2].start()
    blocks(4, 8, b3)
    b2(0, 2)
    delta_dn[1].start()
    b2(2, 2)
    b1(0, 2)
    delta_dn[0].start()
    time_grads(3)
    arrived_delta(2)
    blocks(4, 8, b2)
    time_grads(2)
    b1(2, 2)
    b1(4, 2)
    arrived_delta(1)
    b1(6, 2)
    time_grads(1)
    b0(0, 2)
    b0(2, 2)
    b0(4, 2)
    arrived_delta(0)
    b0(6, 2)

    sd_up = remote(sd.at[:, 192:256], sd_lo, row_sem.at[4], row_sem.at[5], (t, r_next))
    sd_dn = remote(sd.at[:, 0:64], sd_hi, row_sem.at[6], row_sem.at[7], (t, r_prev))
    sd_up.start()
    sd_dn.start()

    def core_copy(g, ra, at):
        return remote(g.at[1 - c], ra, a_sem.at[at], a_sem.at[at + 1], (t, sibling))

    a_t = core_copy(g_t, ra_t, 0)
    a_s = core_copy(g_s, ra_s, 2)

    def z_copies(ma, rb, group):
        return [
            remote(
                ma.at[lax.rem(z + k, 8)], rb.at[z], b_send.at[group, k], b_recv.at[group, z],
                (t, lax.rem(r + 2 * k, 16)),
            )
            for k in range(1, 8)
        ]

    def z_arrival(rb, group, k):
        source = lax.rem(z + 8 - k, 8)
        return remote(
            rb.at[source], rb.at[source], b_send.at[group, k], b_recv.at[group, source],
            (t, lax.rem(r + 16 - 2 * k, 16)),
        )

    def add_cores(copy, g, ra, ma, rb, group):
        copy.wait()

        @pl.loop(0, 8)
        def _(p):
            ma[p] = (g[c, p].astype(F32) + ra[p].astype(F32)).astype(BF)

        copies = z_copies(ma, rb, group)
        for k in (4, 3, 5, 2, 6, 1, 7):
            copies[k - 1].start()
        rb[z] = ma[z]
        return copies

    def add_z(copies, rb, mb, group):
        for k in range(1, 8):
            z_arrival(rb, group, k).wait_recv()
        total = rb[0].astype(F32)
        for p in range(1, 8):
            total = total + rb[p].astype(F32)
        mb[...] = total.astype(BF)
        for copy in copies:
            copy.wait_send()

    def to_owner(taps, mb, rc, group, first):
        for k in range(taps):
            owner = first + k

            @pl.when(t != owner)
            def _():
                remote(
                    mb.at[k], rc.at[t], c_send.at[group, k], c_recv.at[group, t], (owner, r)
                ).start()

    def own_sum(taps, mb, rc, mc, group, first):
        mine = t - first

        @pl.when((t >= first) & (t < first + taps))
        def _():
            rc[t] = mb[mine]
            for k in range(1, 16):
                source = lax.rem(t + k, 16)
                remote(
                    rc.at[source], rc.at[source], c_send.at[group, 0], c_recv.at[group, source],
                    (source, r),
                ).wait_recv()
            total = rc[0].astype(F32)
            for p in range(1, 16):
                total = total + rc[p].astype(F32)
            mc[mine] = total.astype(BF)
            for k in range(1, 16):
                remote(
                    mc.at[mine], mc.at[mine], h_send.at[group, k], h_recv.at[group, mine],
                    (lax.rem(t + k, 16), r),
                ).start()

    def finish(taps, mb, rc, mc, group, first, target):
        mine = t - first
        for k in range(taps):
            owner = first + k

            @pl.when(t != owner)
            def _():
                remote(
                    mb.at[k], rc.at[t], c_send.at[group, k], c_recv.at[group, t], (owner, r)
                ).wait_send()
                remote(
                    mc.at[k], mc.at[k], h_send.at[group, 0], h_recv.at[group, k], (owner, r)
                ).wait_recv()

        target[...] = mc[...].astype(F32) * factor

        @pl.when((t >= first) & (t < first + taps))
        def _():
            for k in range(1, 16):
                remote(
                    mc.at[mine], mc.at[mine], h_send.at[group, k], h_recv.at[group, mine],
                    (lax.rem(t + k, 16), r),
                ).wait_send()

    time_grads(0)
    a_t.start()

    for f in range(F):
        dT[0:256, 256 * f : 256 * f + 256] = sd[f].T

    copies_t = None
    for i in range(3):
        for j in range(3):
            rows = xs[:, 64 * i : 64 * i + 256, 256 * j : 256 * j + 256].reshape(2048, N)
            put(g_s, 3 * i + j, dot(dT[0:256, :], rows))
        if i == 0:
            copies_t = add_cores(a_t, g_t, ra_t, ma_t, rb_t, 0)
    a_s.start()

    @pl.loop(0, F)
    def _(f):
        v = sd[f]
        left, right = columns(v)
        ys[f, 64:320, 0:256] = right
        ys[f, 64:320, 256:512] = v
        ys[f, 64:320, 512:768] = left

    sd_up.wait()
    sd_dn.wait()

    @pl.when(r == 0)
    def _():
        sd_lo[...] = jnp.zeros_like(sd_lo)

    @pl.when(r == 15)
    def _():
        sd_hi[...] = jnp.zeros_like(sd_hi)

    @pl.loop(0, F)
    def _(f):
        for ref, at in ((sd_lo, 0), (sd_hi, 320)):
            v = ref[f]
            left, right = columns(v)
            ys[f, at : at + 64, 0:256] = right
            ys[f, at : at + 64, 256:512] = v
            ys[f, at : at + 64, 512:768] = left

    copies_s = add_cores(a_s, g_s, ra_s, ma_s, rb_s, 1)
    add_z(copies_t, rb_t, mb_t, 0)
    to_owner(8, mb_t, rc_t, 0, 8)

    @pl.loop(0, F // 2)
    def _(b):
        f = 2 * b
        cat = jnp.concatenate(
            [
                ys[pl.ds(f, 2), 64 * (2 - i) : 64 * (2 - i) + 256, :].reshape(512, 768)
                for i in range(3)
            ],
            axis=1,
        )
        total = dot(cat, wsT[...].reshape(2304, 256)) + past(cot, f, 2).astype(F32)
        gin[pl.ds(f, 2)] = total.astype(BF).reshape(2, N, N)

    own_sum(8, mb_t, rc_t, mc_t, 0, 8)
    arrived_state(3)

    @pl.loop(0, F // 2)
    def _(b):
        f = 2 * b
        total = temporal(3, f, 2) + past(lat, f, 2).astype(F32)
        out[pl.ds(f, 2)] = total.astype(BF).reshape(2, N, N)

    add_z(copies_s, rb_s, mb_s, 1)
    to_owner(9, mb_s, rc_s, 1, 0)
    own_sum(9, mb_s, rc_s, mc_s, 1, 0)
    finish(8, mb_t, rc_t, mc_t, 0, 8, gt_out)
    finish(9, mb_s, rc_s, mc_s, 1, 0, gs_out)


def shards(latents, cotangent, w_spatial, w_time):
    shape = latents.shape
    vmem = pl.BlockSpec(memory_space=pltpu.VMEM)
    V = pltpu.VMEM
    scratch = [
        V((F, 384, 768), BF), V((F, 384, 768), BF),
        V((F, 64, N), BF), V((F, 64, N), BF), V((F, 64, N), BF), V((F, 64, N), BF),
        V((9, N, N), BF), V((10, N, N), BF), V((12, N, N), BF), V((16, N, N), BF),
        V((4, F, N, N), F32),
        V((9, N, N), BF), V((10, N, N), BF), V((12, N, N), BF), V((F, N, N), BF), V((F, N, N), BF),
        V((512, 2048), BF), V((3, 768, 256), BF), V((4, 512, 256), BF),
        V((2, 8, 8, 16, N), BF), V((2, 8, 9, 16, N), BF),
        V((8, 8, 16, N), BF), V((8, 9, 16, N), BF),
        V((8, 8, 16, N), BF), V((8, 9, 16, N), BF),
        V((8, 8, 16, N), BF), V((8, 9, 16, N), BF),
        V((8, 16, N), BF), V((9, 16, N), BF),
        V((16, 16, N), BF), V((16, 16, N), BF),
        V((8, 16, N), BF), V((9, 16, N), BF),
        pltpu.SemaphoreType.DMA((8,)), pltpu.SemaphoreType.DMA((16,)),
        pltpu.SemaphoreType.DMA((4,)),
        pltpu.SemaphoreType.DMA((2, 8)), pltpu.SemaphoreType.DMA((2, 8)),
        pltpu.SemaphoreType.DMA((2, 9)), pltpu.SemaphoreType.DMA((2, 16)),
        pltpu.SemaphoreType.DMA((2, 16)), pltpu.SemaphoreType.DMA((2, 9)),
    ]
    out, gin, gs, gt = pl.pallas_call(
        kernel,
        out_shape=[
            jax.ShapeDtypeStruct((F, N, N), BF),
            jax.ShapeDtypeStruct((F, N, N), BF),
            jax.ShapeDtypeStruct((9, 16, N), F32),
            jax.ShapeDtypeStruct((8, 16, N), F32),
        ],
        in_specs=[vmem] * 4,
        out_specs=[vmem] * 4,
        scratch_shapes=scratch,
        compiler_params=pltpu.CompilerParams(
            collective_id=0, has_side_effects=True, vmem_limit_bytes=60 * 1024 * 1024
        ),
        cost_estimate=pl.CostEstimate(
            flops=51 * 2 * 2048 * N * N, bytes_accessed=7 * 1024 * 1024, transcendentals=4 * 2048 * N
        ),
    )(
        latents.reshape(F, N, N), cotangent.reshape(F, N, N),
        w_spatial.reshape(3, 768, N), w_time.reshape(4, 512, N),
    )
    spatial = jnp.swapaxes(gs, 1, 2)
    time = jnp.swapaxes(gt, 1, 2).reshape(4, 2, N, 16)
    return out.reshape(shape), gin.reshape(shape), spatial, time


def solution(mesh):
    in_specs = (P("tm", "rows", None, None), P("tm", "rows", None, None), P(), P())
    out_specs = (
        P("tm", "rows", None, None),
        P("tm", "rows", None, None),
        P(None, None, "rows"),
        P(None, None, None, "rows"),
    )
    return jax.shard_map(shards, mesh=mesh, in_specs=in_specs, out_specs=out_specs, check_vma=False)
```

```python
import math

import jax
import jax.numpy as jnp
from jax import lax
from jax.experimental import pallas as pl
from jax.experimental.pallas import tpu as pltpu
from jax.sharding import PartitionSpec as P

MESH = pl.DeviceIdType.MESH
F = 8
N = 256
HALF = 128
BF = jnp.bfloat16
F32 = jnp.float32


def dot(a, b):
    return lax.dot_general(a, b, (((1,), (0,)), ((), ())), preferred_element_type=F32)


def columns(v):
    wide = v.astype(F32)
    n = wide.shape[0]
    col = lax.rem(lax.broadcasted_iota(jnp.int32, wide.shape, 0), 64)
    left = jnp.where(col == 0, 0.0, pltpu.roll(wide, 1, 0)).astype(BF)
    right = jnp.where(col == 63, 0.0, pltpu.roll(wide, n - 1, 0)).astype(BF)
    return left, right


def kernel(
    lat_in, cot_in, ws_in, wt_in,
    out_hbm, gin_hbm, gs_out, gt_out,
    lat, cot, ws, wt, out, gin,
    xs, ys, lat_lo, lat_hi, sd_lo, sd_hi,
    s0, s1, s2, s3, slope, d0, d1, d2, d3h, sd, dT, wsT, wtT,
    g_a, g_b, g_x, g_y, g_z,
    ra_a, ra_b, ra_x, ra_y, ra_z,
    ma_a, ma_b, ma_x, ma_y, ma_z,
    rb_a, rb_b, rb_x, rb_y, rb_z,
    mb_t, mb_s, rc_t, rc_s, mc_t, mc_s,
    load_sem, row_sem, tm_send, tm_recv, a_sem, b_send, b_recv, c_send, c_recv, h_send, h_recv,
):
    t = lax.axis_index("tm")
    r = lax.axis_index("rows")
    z = r // 2
    c = lax.rem(r, 2)
    tm_next = lax.rem(t + 1, 16)
    tm_prev = lax.rem(t + 15, 16)
    r_next = lax.rem(r + 1, 16)
    r_prev = lax.rem(r + 15, 16)
    sibling = r + 1 - 2 * c
    far = lax.rem(r + 15 + 2 * c, 16)
    states = (s0, s1, s2, s3)
    deltas = (d0, d1, d2, d3h)
    factor = 1.0 / math.sqrt(524288.0)
    barrier = pltpu.get_barrier_semaphore()
    for k in (1, 15, 2, 14, 3, 13, 4, 12, 5, 11, 6, 10, 7, 9, 8):
        pl.semaphore_signal(barrier, inc=1, device_id=(lax.rem(t + k, 16), r), device_id_type=MESH)
    for k in range(1, 8):
        pl.semaphore_signal(
            barrier, inc=1, device_id=(t, lax.rem(r + 2 * k, 16)), device_id_type=MESH
        )
    pl.semaphore_signal(barrier, inc=1, device_id=(t, sibling), device_id_type=MESH)
    pl.semaphore_signal(barrier, inc=1, device_id=(t, far), device_id_type=MESH)

    loads = [
        pltpu.make_async_copy(src, dst, load_sem.at[k])
        for k, (src, dst) in enumerate(((lat_in, lat), (ws_in, ws), (wt_in, wt), (cot_in, cot)))
    ]
    for copy in loads:
        copy.start()
    pl.semaphore_wait(barrier, 24)

    def remote(src, dst, send, recv, device):
        return pltpu.make_async_remote_copy(
            src_ref=src, dst_ref=dst, send_sem=send, recv_sem=recv, device_id=device,
            device_id_type=MESH,
        )
    lat_up = remote(lat_in.at[:, 192:256], lat_lo, row_sem.at[0], row_sem.at[1], (t, r_next))
    lat_dn = remote(lat_in.at[:, 0:64], lat_hi, row_sem.at[2], row_sem.at[3], (t, r_prev))
    lat_up.start()
    lat_dn.start()

    def half(q):
        return slice(HALF * q, HALF * q + HALF)

    state_up = [
        [
            remote(
                states[k].at[8 : 8 + 2**k, half(q)], states[k].at[0 : 2**k, half(q)],
                tm_send.at[q, k], tm_recv.at[q, k], (tm_next, r),
            )
            for k in range(4)
        ]
        for q in range(2)
    ]
    delta_dn = [
        [
            remote(
                deltas[k].at[0 : 2**k, half(q)], deltas[k].at[8 : 8 + 2**k, half(q)],
                tm_send.at[q, 4 + k], tm_recv.at[q, 4 + k], (tm_prev, r),
            )
            for k in range(3)
        ]
        + [
            remote(
                cot_in.at[:, half(q)], d3h.at[:, half(q)], tm_send.at[q, 7], tm_recv.at[q, 7],
                (tm_prev, r),
            )
        ]
        for q in range(2)
    ]
    delta_dn[0][3].start()
    delta_dn[1][3].start()

    loads[0].wait()

    @pl.loop(0, F)
    def _(f):
        v = lat[f]
        left, right = columns(v)
        xs[f, 64:320, 0:256] = left
        xs[f, 64:320, 256:512] = v
        xs[f, 64:320, 512:768] = right

    loads[1].wait()
    lat_up.wait()
    lat_dn.wait()

    @pl.when(r == 0)
    def _():
        lat_lo[...] = jnp.zeros_like(lat_lo)

    @pl.when(r == 15)
    def _():
        lat_hi[...] = jnp.zeros_like(lat_hi)

    @pl.loop(0, F)
    def _(f):
        for ref, at in ((lat_lo, 0), (lat_hi, 320)):
            v = ref[f]
            left, right = columns(v)
            xs[f, at : at + 64, 0:256] = left
            xs[f, at : at + 64, 256:512] = v
            xs[f, at : at + 64, 512:768] = right

    def activate(k, f, n, q, v):
        sigma = 0.5 + 0.5 * jnp.tanh(0.5 * v)
        state = v * sigma
        states[k][2**k + f : 2**k + f + n, half(q)] = state.astype(BF).reshape(n, HALF, N)
        slope[k, f : f + n, half(q)] = (sigma + state * (1.0 - sigma)).reshape(n, HALF, N)

    def conv(f, n, q):
        cat = jnp.concatenate(
            [
                xs[f : f + n, 64 * i + HALF * q : 64 * i + HALF * q + HALF, :].reshape(n * HALF, 768)
                for i in range(3)
            ],
            axis=1,
        )
        activate(0, f, n, q, dot(cat, ws[...].reshape(2304, 256)))

    def past(ref, at, n, q):
        return ref[at : at + n, half(q)].reshape(n * HALF, N)

    def temporal(k, f, n, q):
        cat = jnp.concatenate(
            [past(states[k], f + 2**k, n, q), past(states[k], f, n, q)], axis=1
        )
        return dot(cat, wt[k])

    def forward(k, f, n, q):
        activate(k + 1, f, n, q, temporal(k, f, n, q))

    def arrived_state(k, q):
        state_up[q][k].wait()

        @pl.when(t == 0)
        def _():
            states[k][0 : 2**k, half(q)] = jnp.zeros((2**k, HALF, N), BF)
    for q in range(2):
        conv(4, 4, q)
        state_up[q][0].start()
        conv(0, 4, q)
        if q == 0:
            loads[2].wait()
        forward(0, 4, 4, q)
        state_up[q][1].start()
        forward(0, 1, 3, q)
        forward(1, 4, 4, q)
        state_up[q][2].start()
        forward(1, 3, 1, q)
    for i in range(3):
        for j in range(3):
            wsT[i, 256 * j : 256 * j + 256, :] = ws[i, 256 * j : 256 * j + 256, :].T

    @pl.loop(0, 4)
    def _(k):
        wtT[k, 0:256, :] = wt[k, 0:256, :].T
        wtT[k, 256:512, :] = wt[k, 256:512, :].T

    loads[3].wait()

    def back(k, f, n, q):
        source = cot if k == 3 else deltas[k]
        later = past(d3h, f, n, q) if k == 3 else past(deltas[k], f + 2**k, n, q)
        total = dot(jnp.concatenate([past(source, f, n, q), later], axis=1), wtT[k])
        value = (total * past(slope.at[k], f, n, q)).astype(BF)
        target = sd if k == 0 else deltas[k - 1]
        target[f : f + n, half(q)] = value.reshape(n, HALF, N)

    def arrived_delta(k, q):
        delta_dn[q][k].wait()
        at = 0 if k == 3 else 8

        @pl.when(t == 15)
        def _():
            deltas[k][at : at + 2**k, half(q)] = jnp.zeros((2**k, HALF, N), BF)

    for q in range(2):
        arrived_state(0, q)
        forward(0, 0, 1, q)
        arrived_state(1, q)
        forward(1, 0, 3, q)
        forward(2, 4, 4, q)
        arrived_state(2, q)
        forward(2, 0, 4, q)
        state_up[q][3].start()
        arrived_delta(3, q)
        back(3, 0, 4, q)
        delta_dn[q][2].start()
        back(3, 4, 4, q)
        back(2, 0, 4, q)
        delta_dn[q][1].start()
        back(1, 0, 2, q)
        delta_dn[q][0].start()

    def put(ref, tap, value):
        for part in range(16):
            ref[part % 2, part // 2, tap] = value[16 * part : 16 * part + 16].astype(BF)

    def time_grads(k, ref, tap):
        d = 2**k
        for f in range(F):
            src = cot if k == 3 else deltas[k]
            dT[0:256, 256 * f : 256 * f + 256] = src[f].T
            other = d3h[f] if k == 3 else deltas[k][f + d]
            dT[256:512, 256 * f : 256 * f + 256] = other.T
        both = dot(dT[...], states[k][d : d + F].reshape(2048, N))
        put(ref, tap, both[0:256])
        put(ref, tap + 1, both[256:512])

    groups = [
        (g_a, ra_a, ma_a, rb_a), (g_b, ra_b, ma_b, rb_b),
        (g_x, ra_x, ma_x, rb_x), (g_y, ra_y, ma_y, rb_y), (g_z, ra_z, ma_z, rb_z),
    ]
    between = [
        remote(g.at[1 - c], ra, a_sem.at[n, 0], a_sem.at[n, 1], (t, sibling))
        for n, (g, ra, _, _) in enumerate(groups)
    ]

    def z_copies(n):
        _, _, ma, rb = groups[n]
        return [
            remote(
                ma.at[lax.rem(z + k, 8)], rb.at[z], b_send.at[n, k], b_recv.at[n, z],
                (t, lax.rem(r + 2 * k, 16)),
            )
            for k in (4, 3, 5, 2, 6, 1, 7)
        ]

    def add_cores(n):
        g, ra, ma, rb = groups[n]
        between[n].wait()

        @pl.loop(0, 8)
        def _(p):
            ma[p] = (g[c, p].astype(F32) + ra[p].astype(F32)).astype(BF)

        for copy in z_copies(n):
            copy.start()
        rb[z] = ma[z]

    def add_z(n, mb, at):
        taps = groups[n][0].shape[2]
        rb = groups[n][3]
        for k in range(1, 8):
            source = lax.rem(z + 8 - k, 8)
            remote(
                rb.at[source], rb.at[source], b_send.at[n, k], b_recv.at[n, source],
                (t, lax.rem(r + 16 - 2 * k, 16)),
            ).wait_recv()
        total = rb[0].astype(F32)
        for p in range(1, 8):
            total = total + rb[p].astype(F32)
        mb[at : at + taps] = total.astype(BF)

    def sent_z(n):
        for copy in z_copies(n):
            copy.wait_send()

    def to_owner(low, high, mb, rc, group, first):
        for k in range(low, high):
            owner = first + k

            @pl.when(t != owner)
            def _():
                remote(
                    mb.at[k], rc.at[t], c_send.at[group, k], c_recv.at[group, t], (owner, r)
                ).start()

    def own_sum(taps, mb, rc, mc, group, first):
        mine = t - first

        @pl.when((t >= first) & (t < first + taps))
        def _():
            rc[t] = mb[mine]
            for k in range(1, 16):
                source = lax.rem(t + k, 16)
                remote(
                    rc.at[source], rc.at[source], c_send.at[group, 0], c_recv.at[group, source],
                    (source, r),
                ).wait_recv()
            total = rc[0].astype(F32)
            for p in range(1, 16):
                total = total + rc[p].astype(F32)
            mc[mine] = total.astype(BF)
            for k in range(1, 16):
                remote(
                    mc.at[mine], mc.at[mine], h_send.at[group, k], h_recv.at[group, mine],
                    (lax.rem(t + k, 16), r),
                ).start()

    def finish(taps, mb, rc, mc, group, first, target):
        mine = t - first
        for k in range(taps):
            owner = first + k

            @pl.when(t != owner)
            def _():
                remote(
                    mb.at[k], rc.at[t], c_send.at[group, k], c_recv.at[group, t], (owner, r)
                ).wait_send()
                remote(
                    mc.at[k], mc.at[k], h_send.at[group, 0], h_recv.at[group, k], (owner, r)
                ).wait_recv()

        target[...] = mc[...].astype(F32) * factor

        @pl.when((t >= first) & (t < first + taps))
        def _():
            for k in range(1, 16):
                remote(
                    mc.at[mine], mc.at[mine], h_send.at[group, k], h_recv.at[group, mine],
                    (lax.rem(t + k, 16), r),
                ).wait_send()
    time_grads(3, g_a, 2)
    arrived_delta(2, 0)
    back(2, 4, 4, 0)
    back(1, 2, 2, 0)
    arrived_delta(1, 0)
    back(1, 4, 4, 0)
    back(0, 0, 4, 0)
    arrived_delta(0, 0)
    back(0, 4, 4, 0)
    sd_dn = remote(sd.at[:, 0:64], sd_hi, row_sem.at[6], row_sem.at[7], (t, r_prev))
    sd_dn.start()
    arrived_delta(2, 1)
    back(2, 4, 4, 1)
    time_grads(2, g_a, 0)
    between[0].start()
    back(1, 2, 2, 1)
    arrived_delta(1, 1)
    back(1, 4, 4, 1)
    back(0, 0, 4, 1)
    add_cores(0)
    arrived_delta(0, 1)
    back(0, 4, 4, 1)
    sd_up = remote(sd.at[:, 192:256], sd_lo, row_sem.at[4], row_sem.at[5], (t, r_next))
    sd_up.start()

    def spatial_grads(i, ref):
        rows = xs[:, 64 * i : 64 * i + 256, :].reshape(2048, 768)
        total = dot(dT[0:256, :], rows)
        for j in range(3):
            put(ref, j, total[:, 256 * j : 256 * j + 256])

    for f in range(F):
        dT[0:256, 256 * f : 256 * f + 256] = sd[f].T
    spatial_grads(0, g_x)
    between[2].start()
    spatial_grads(1, g_y)
    between[3].start()
    add_cores(2)
    spatial_grads(2, g_z)
    between[4].start()
    add_cores(3)
    time_grads(1, g_b, 2)
    add_cores(4)
    time_grads(0, g_b, 0)
    between[1].start()

    @pl.loop(0, F)
    def _(f):
        v = sd[f]
        left, right = columns(v)
        ys[f, 64:320, 0:256] = right
        ys[f, 64:320, 256:512] = v
        ys[f, 64:320, 512:768] = left

    add_cores(1)
    sd_up.wait()
    sd_dn.wait()

    @pl.when(r == 0)
    def _():
        sd_lo[...] = jnp.zeros_like(sd_lo)

    @pl.when(r == 15)
    def _():
        sd_hi[...] = jnp.zeros_like(sd_hi)

    @pl.loop(0, F)
    def _(f):
        for ref, at in ((sd_lo, 0), (sd_hi, 320)):
            v = ref[f]
            left, right = columns(v)
            ys[f, at : at + 64, 0:256] = right
            ys[f, at : at + 64, 256:512] = v
            ys[f, at : at + 64, 512:768] = left
    def input_grads(f, n, q):
        cat = jnp.concatenate(
            [
                ys[f : f + n, 64 * (2 - i) + HALF * q : 64 * (2 - i) + HALF * q + HALF, :].reshape(
                    n * HALF, 768
                )
                for i in range(3)
            ],
            axis=1,
        )
        total = dot(cat, wsT[...].reshape(2304, 256)) + past(cot, f, n, q).astype(F32)
        gin[f : f + n, half(q)] = total.astype(BF).reshape(n, HALF, N)

    def outputs(f, n, q):
        total = temporal(3, f, n, q) + past(lat, f, n, q).astype(F32)
        out[f : f + n, half(q)] = total.astype(BF).reshape(n, HALF, N)

    input_grads(0, 4, 0)
    input_grads(4, 4, 0)
    add_z(0, mb_t, 4)
    to_owner(4, 8, mb_t, rc_t, 0, 8)
    input_grads(0, 4, 1)
    input_grads(4, 4, 1)
    gin_store = pltpu.make_async_copy(gin, gin_hbm, load_sem.at[4])
    gin_store.start()
    add_z(2, mb_s, 0)
    to_owner(0, 3, mb_s, rc_s, 1, 0)
    for q in range(2):
        arrived_state(3, q)
        outputs(0, 4, q)
        outputs(4, 4, q)
    out_store = pltpu.make_async_copy(out, out_hbm, load_sem.at[5])
    out_store.start()
    add_z(3, mb_s, 3)
    to_owner(3, 6, mb_s, rc_s, 1, 0)
    add_z(4, mb_s, 6)
    to_owner(6, 9, mb_s, rc_s, 1, 0)
    add_z(1, mb_t, 0)
    to_owner(0, 4, mb_t, rc_t, 0, 8)
    own_sum(9, mb_s, rc_s, mc_s, 1, 0)
    own_sum(8, mb_t, rc_t, mc_t, 0, 8)
    for n in range(5):
        sent_z(n)
    finish(9, mb_s, rc_s, mc_s, 1, 0, gs_out)
    finish(8, mb_t, rc_t, mc_t, 0, 8, gt_out)
    gin_store.wait()
    out_store.wait()
def handed_on(*refs):
    sem = refs[-1]
    copies = [
        pltpu.make_async_copy(refs[k], refs[4 + k], sem.at[k]) for k in range(4)
    ]
    for copy in copies:
        copy.start()
    for copy in copies:
        copy.wait()


def shards(latents, cotangent, w_spatial, w_time):
    shape = latents.shape
    vmem = pl.BlockSpec(memory_space=pltpu.VMEM)
    hbm = pl.BlockSpec(memory_space=pl.ANY)
    V = pltpu.VMEM
    DMA = pltpu.SemaphoreType.DMA
    sizes = (4, 4, 3, 3, 3)
    scratch = [
        V((F, N, N), BF), V((F, N, N), BF), V((3, 768, N), BF), V((4, 512, N), BF),
        V((F, N, N), BF), V((F, N, N), BF),
        V((F, 384, 768), BF), V((F, 384, 768), BF),
        V((F, 64, N), BF), V((F, 64, N), BF), V((F, 64, N), BF), V((F, 64, N), BF),
        V((9, N, N), BF), V((10, N, N), BF), V((12, N, N), BF), V((16, N, N), BF),
        V((4, F, N, N), F32),
        V((9, N, N), BF), V((10, N, N), BF), V((12, N, N), BF), V((F, N, N), BF), V((F, N, N), BF),
        V((512, 2048), BF), V((3, 768, 256), BF), V((4, 512, 256), BF),
        *[V((2, 8, n, 16, N), BF) for n in sizes],
        *[V((8, n, 16, N), BF) for n in sizes],
        *[V((8, n, 16, N), BF) for n in sizes],
        *[V((8, n, 16, N), BF) for n in sizes],
        V((8, 16, N), BF), V((9, 16, N), BF),
        V((16, 16, N), BF), V((16, 16, N), BF),
        V((8, 16, N), BF), V((9, 16, N), BF),
        DMA((6,)), DMA((8,)), DMA((2, 8)), DMA((2, 8)), DMA((5, 2)),
        DMA((5, 8)), DMA((5, 8)), DMA((2, 9)), DMA((2, 16)), DMA((2, 16)), DMA((2, 9)),
    ]
    results = [
        jax.ShapeDtypeStruct((F, N, N), BF),
        jax.ShapeDtypeStruct((F, N, N), BF),
        jax.ShapeDtypeStruct((9, 16, N), F32),
        jax.ShapeDtypeStruct((8, 16, N), F32),
    ]
    held = pl.pallas_call(
        kernel,
        out_shape=results,
        in_specs=[hbm] * 4,
        out_specs=[hbm, hbm, vmem, vmem],
        scratch_shapes=scratch,
        compiler_params=pltpu.CompilerParams(
            collective_id=0, has_side_effects=True, vmem_limit_bytes=60 * 1024 * 1024
        ),
        cost_estimate=pl.CostEstimate(
            flops=51 * 2 * 2048 * N * N, bytes_accessed=7 * 1024 * 1024, transcendentals=4 * 2048 * N
        ),
    )(
        latents.reshape(F, N, N), cotangent.reshape(F, N, N),
        w_spatial.reshape(3, 768, N), w_time.reshape(4, 512, N),
    )
    out, gin, gs, gt = pl.pallas_call(
        handed_on,
        out_shape=results,
        in_specs=[hbm] * 4,
        out_specs=[hbm] * 4,
        scratch_shapes=[DMA((4,))],
        cost_estimate=pl.CostEstimate(flops=0, bytes_accessed=5 * 1024 * 1024, transcendentals=0),
    )(*held)
    spatial = jnp.swapaxes(gs, 1, 2)
    time = jnp.swapaxes(gt, 1, 2).reshape(4, 2, N, 16)
    return out.reshape(shape), gin.reshape(shape), spatial, time


def solution(mesh):
    in_specs = (P("tm", "rows", None, None), P("tm", "rows", None, None), P(), P())
    out_specs = (
        P("tm", "rows", None, None),
        P("tm", "rows", None, None),
        P(None, None, "rows"),
        P(None, None, None, "rows"),
    )
    return jax.shard_map(shards, mesh=mesh, in_specs=in_specs, out_specs=out_specs, check_vma=False)
```

```python
import math

import jax
import jax.numpy as jnp
from jax import lax
from jax.experimental import pallas as pl
from jax.experimental.pallas import tpu as pltpu
from jax.sharding import PartitionSpec as P

MESH = pl.DeviceIdType.MESH
F = 8
N = 256
HALF = 128
BF = jnp.bfloat16
F32 = jnp.float32


def dot(a, b):
    return lax.dot_general(a, b, (((1,), (0,)), ((), ())), preferred_element_type=F32)


def columns(v):
    wide = v.astype(F32)
    n = wide.shape[0]
    col = lax.rem(lax.broadcasted_iota(jnp.int32, wide.shape, 0), 64)
    left = jnp.where(col == 0, 0.0, pltpu.roll(wide, 1, 0)).astype(BF)
    right = jnp.where(col == 63, 0.0, pltpu.roll(wide, n - 1, 0)).astype(BF)
    return left, right


def kernel(
    lat_in, cot_in, ws_in, wt_in,
    out_hbm, gin_hbm, gs_out, gt_out,
    lat, cot, ws, wt, out, gin,
    xs, ys, lat_lo, lat_hi, sd_lo, sd_hi,
    s0, s1, s2, s3, slope, d0, d1, d2, d3h, sd, dT, wsT, wtT,
    g_a, g_b, g_x, g_y, g_z,
    ra_a, ra_b, ra_x, ra_y, ra_z,
    ma_a, ma_b, ma_x, ma_y, ma_z,
    rb_a, rb_b, rb_x, rb_y, rb_z,
    mb_t, mb_s, rc_t, rc_s, mc_t, mc_s,
    load_sem, row_sem, tm_send, tm_recv, a_sem, b_send, b_recv, c_send, c_recv, h_send, h_recv,
):
    t = lax.axis_index("tm")
    r = lax.axis_index("rows")
    z = r // 2
    c = lax.rem(r, 2)
    tm_next = lax.rem(t + 1, 16)
    tm_prev = lax.rem(t + 15, 16)
    r_next = lax.rem(r + 1, 16)
    r_prev = lax.rem(r + 15, 16)
    sibling = r + 1 - 2 * c
    far = lax.rem(r + 15 + 2 * c, 16)
    states = (s0, s1, s2, s3)
    deltas = (d0, d1, d2, d3h)
    factor = 1.0 / math.sqrt(524288.0)
    barrier = pltpu.get_barrier_semaphore()
    for k in (1, 15, 2, 14, 3, 13, 4, 12, 5, 11, 6, 10, 7, 9, 8):
        pl.semaphore_signal(barrier, inc=1, device_id=(lax.rem(t + k, 16), r), device_id_type=MESH)
    for k in range(1, 8):
        pl.semaphore_signal(
            barrier, inc=1, device_id=(t, lax.rem(r + 2 * k, 16)), device_id_type=MESH
        )
    pl.semaphore_signal(barrier, inc=1, device_id=(t, sibling), device_id_type=MESH)
    pl.semaphore_signal(barrier, inc=1, device_id=(t, far), device_id_type=MESH)

    loads = [
        pltpu.make_async_copy(src, dst, load_sem.at[k])
        for k, (src, dst) in enumerate(((lat_in, lat), (ws_in, ws), (wt_in, wt), (cot_in, cot)))
    ]
    for copy in loads:
        copy.start()
    pl.semaphore_wait(barrier, 24)

    def remote(src, dst, send, recv, device):
        return pltpu.make_async_remote_copy(
            src_ref=src, dst_ref=dst, send_sem=send, recv_sem=recv, device_id=device,
            device_id_type=MESH,
        )
    lat_up = remote(lat_in.at[:, 192:256], lat_lo, row_sem.at[0], row_sem.at[1], (t, r_next))
    lat_dn = remote(lat_in.at[:, 0:64], lat_hi, row_sem.at[2], row_sem.at[3], (t, r_prev))
    lat_up.start()
    lat_dn.start()

    def half(q):
        return slice(HALF * q, HALF * q + HALF)

    state_up = [
        [
            remote(
                states[k].at[8 : 8 + 2**k, half(q)], states[k].at[0 : 2**k, half(q)],
                tm_send.at[q, k], tm_recv.at[q, k], (tm_next, r),
            )
            for k in range(4)
        ]
        for q in range(2)
    ]
    delta_dn = [
        [
            remote(
                deltas[k].at[0 : 2**k, half(q)], deltas[k].at[8 : 8 + 2**k, half(q)],
                tm_send.at[q, 4 + k], tm_recv.at[q, 4 + k], (tm_prev, r),
            )
            for k in range(3)
        ]
        + [
            remote(
                cot_in.at[:, half(q)], d3h.at[:, half(q)], tm_send.at[q, 7], tm_recv.at[q, 7],
                (tm_prev, r),
            )
        ]
        for q in range(2)
    ]
    delta_dn[0][3].start()
    delta_dn[1][3].start()

    loads[0].wait()

    @pl.loop(0, F)
    def _(f):
        v = lat[f]
        left, right = columns(v)
        xs[f, 64:320, 0:256] = left
        xs[f, 64:320, 256:512] = v
        xs[f, 64:320, 512:768] = right

    loads[1].wait()
    lat_up.wait()
    lat_dn.wait()

    @pl.when(r == 0)
    def _():
        lat_lo[...] = jnp.zeros_like(lat_lo)

    @pl.when(r == 15)
    def _():
        lat_hi[...] = jnp.zeros_like(lat_hi)

    @pl.loop(0, F)
    def _(f):
        for ref, at in ((lat_lo, 0), (lat_hi, 320)):
            v = ref[f]
            left, right = columns(v)
            xs[f, at : at + 64, 0:256] = left
            xs[f, at : at + 64, 256:512] = v
            xs[f, at : at + 64, 512:768] = right

    def activate(k, f, n, q, v):
        sigma = 0.5 + 0.5 * jnp.tanh(0.5 * v)
        state = v * sigma
        states[k][2**k + f : 2**k + f + n, half(q)] = state.astype(BF).reshape(n, HALF, N)
        slope[k, f : f + n, half(q)] = (sigma + state * (1.0 - sigma)).reshape(n, HALF, N)

    def conv(f, n, q):
        cat = jnp.concatenate(
            [
                xs[f : f + n, 64 * i + HALF * q : 64 * i + HALF * q + HALF, :].reshape(n * HALF, 768)
                for i in range(3)
            ],
            axis=1,
        )
        activate(0, f, n, q, dot(cat, ws[...].reshape(2304, 256)))

    def past(ref, at, n, q):
        return ref[at : at + n, half(q)].reshape(n * HALF, N)

    def temporal(k, f, n, q):
        cat = jnp.concatenate(
            [past(states[k], f + 2**k, n, q), past(states[k], f, n, q)], axis=1
        )
        return dot(cat, wt[k])

    def forward(k, f, n, q):
        activate(k + 1, f, n, q, temporal(k, f, n, q))

    def arrived_state(k, q):
        state_up[q][k].wait()

        @pl.when(t == 0)
        def _():
            states[k][0 : 2**k, half(q)] = jnp.zeros((2**k, HALF, N), BF)
    for q in range(2):
        conv(4, 4, q)
        state_up[q][0].start()
        conv(0, 4, q)
        if q == 0:
            loads[2].wait()
        forward(0, 4, 4, q)
        state_up[q][1].start()
        forward(0, 1, 3, q)
        forward(1, 4, 4, q)
        state_up[q][2].start()
        forward(1, 3, 1, q)
    for i in range(3):
        for j in range(3):
            wsT[i, 256 * j : 256 * j + 256, :] = ws[i, 256 * j : 256 * j + 256, :].T

    @pl.loop(0, 4)
    def _(k):
        wtT[k, 0:256, :] = wt[k, 0:256, :].T
        wtT[k, 256:512, :] = wt[k, 256:512, :].T

    loads[3].wait()

    def back(k, f, n, q):
        source = cot if k == 3 else deltas[k]
        later = past(d3h, f, n, q) if k == 3 else past(deltas[k], f + 2**k, n, q)
        total = dot(jnp.concatenate([past(source, f, n, q), later], axis=1), wtT[k])
        value = (total * past(slope.at[k], f, n, q)).astype(BF)
        target = sd if k == 0 else deltas[k - 1]
        target[f : f + n, half(q)] = value.reshape(n, HALF, N)

    def arrived_delta(k, q):
        delta_dn[q][k].wait()
        at = 0 if k == 3 else 8

        @pl.when(t == 15)
        def _():
            deltas[k][at : at + 2**k, half(q)] = jnp.zeros((2**k, HALF, N), BF)

    for q in range(2):
        arrived_state(0, q)
        forward(0, 0, 1, q)
        arrived_state(1, q)
        forward(1, 0, 3, q)
        forward(2, 4, 4, q)
        arrived_state(2, q)
        forward(2, 0, 4, q)
        state_up[q][3].start()
        arrived_delta(3, q)
        back(3, 0, 4, q)
        delta_dn[q][2].start()
        back(3, 4, 4, q)
        back(2, 0, 4, q)
        delta_dn[q][1].start()
        back(1, 0, 2, q)
        delta_dn[q][0].start()

    def put(ref, tap, value):
        for part in range(16):
            ref[part % 2, part // 2, tap] = value[16 * part : 16 * part + 16].astype(BF)

    def time_grads(k, ref, tap):
        d = 2**k
        for f in range(F):
            src = cot if k == 3 else deltas[k]
            dT[0:256, 256 * f : 256 * f + 256] = src[f].T
            other = d3h[f] if k == 3 else deltas[k][f + d]
            dT[256:512, 256 * f : 256 * f + 256] = other.T
        both = dot(dT[...], states[k][d : d + F].reshape(2048, N))
        put(ref, tap, both[0:256])
        put(ref, tap + 1, both[256:512])

    groups = [
        (g_a, ra_a, ma_a, rb_a), (g_b, ra_b, ma_b, rb_b),
        (g_x, ra_x, ma_x, rb_x), (g_y, ra_y, ma_y, rb_y), (g_z, ra_z, ma_z, rb_z),
    ]
    between = [
        remote(g.at[1 - c], ra, a_sem.at[n, 0], a_sem.at[n, 1], (t, sibling))
        for n, (g, ra, _, _) in enumerate(groups)
    ]

    def z_copies(n):
        _, _, ma, rb = groups[n]
        return [
            remote(
                ma.at[lax.rem(z + k, 8)], rb.at[z], b_send.at[n, k], b_recv.at[n, z],
                (t, lax.rem(r + 2 * k, 16)),
            )
            for k in (4, 3, 5, 2, 6, 1, 7)
        ]

    def add_cores(n):
        g, ra, ma, rb = groups[n]
        between[n].wait()

        @pl.loop(0, 8)
        def _(p):
            ma[p] = (g[c, p].astype(F32) + ra[p].astype(F32)).astype(BF)

        for copy in z_copies(n):
            copy.start()
        rb[z] = ma[z]

    def add_z(n, mb, at):
        taps = groups[n][0].shape[2]
        rb = groups[n][3]
        for k in range(1, 8):
            source = lax.rem(z + 8 - k, 8)
            remote(
                rb.at[source], rb.at[source], b_send.at[n, k], b_recv.at[n, source],
                (t, lax.rem(r + 16 - 2 * k, 16)),
            ).wait_recv()
        total = rb[0].astype(F32)
        for p in range(1, 8):
            total = total + rb[p].astype(F32)
        mb[at : at + taps] = total.astype(BF)

    def sent_z(n):
        for copy in z_copies(n):
            copy.wait_send()

    def to_owner(low, high, mb, rc, group, first):
        for k in range(low, high):
            owner = first + k

            @pl.when(t != owner)
            def _():
                remote(
                    mb.at[k], rc.at[t], c_send.at[group, k], c_recv.at[group, t], (owner, r)
                ).start()

    def own_sum(taps, mb, rc, mc, group, first):
        mine = t - first

        @pl.when((t >= first) & (t < first + taps))
        def _():
            rc[t] = mb[mine]
            for k in range(1, 16):
                source = lax.rem(t + k, 16)
                remote(
                    rc.at[source], rc.at[source], c_send.at[group, 0], c_recv.at[group, source],
                    (source, r),
                ).wait_recv()
            total = rc[0].astype(F32)
            for p in range(1, 16):
                total = total + rc[p].astype(F32)
            mc[mine] = total.astype(BF)
            for k in range(1, 16):
                remote(
                    mc.at[mine], mc.at[mine], h_send.at[group, k], h_recv.at[group, mine],
                    (lax.rem(t + k, 16), r),
                ).start()

    def finish(taps, mb, rc, mc, group, first, target):
        mine = t - first
        for k in range(taps):
            owner = first + k

            @pl.when(t != owner)
            def _():
                remote(
                    mb.at[k], rc.at[t], c_send.at[group, k], c_recv.at[group, t], (owner, r)
                ).wait_send()
                remote(
                    mc.at[k], mc.at[k], h_send.at[group, 0], h_recv.at[group, k], (owner, r)
                ).wait_recv()

        target[...] = mc[...].astype(F32) * factor

        @pl.when((t >= first) & (t < first + taps))
        def _():
            for k in range(1, 16):
                remote(
                    mc.at[mine], mc.at[mine], h_send.at[group, k], h_recv.at[group, mine],
                    (lax.rem(t + k, 16), r),
                ).wait_send()
    time_grads(3, g_a, 2)
    arrived_delta(2, 0)
    back(2, 4, 4, 0)
    back(1, 2, 2, 0)
    arrived_delta(1, 0)
    back(1, 4, 4, 0)
    back(0, 0, 4, 0)
    arrived_delta(0, 0)
    back(0, 4, 4, 0)
    sd_dn = remote(sd.at[:, 0:64], sd_hi, row_sem.at[6], row_sem.at[7], (t, r_prev))
    sd_dn.start()
    arrived_delta(2, 1)
    back(2, 4, 4, 1)
    time_grads(2, g_a, 0)
    between[0].start()
    back(1, 2, 2, 1)
    arrived_delta(1, 1)
    back(1, 4, 4, 1)
    back(0, 0, 4, 1)
    add_cores(0)
    arrived_delta(0, 1)
    back(0, 4, 4, 1)
    sd_up = remote(sd.at[:, 192:256], sd_lo, row_sem.at[4], row_sem.at[5], (t, r_next))
    sd_up.start()

    def spatial_grads(i, ref):
        rows = xs[:, 64 * i : 64 * i + 256, :].reshape(2048, 768)
        total = dot(dT[0:256, :], rows)
        for j in range(3):
            put(ref, j, total[:, 256 * j : 256 * j + 256])

    for f in range(F):
        dT[0:256, 256 * f : 256 * f + 256] = sd[f].T
    spatial_grads(0, g_x)
    between[2].start()
    spatial_grads(1, g_y)
    between[3].start()
    add_cores(2)
    spatial_grads(2, g_z)
    between[4].start()
    add_cores(3)
    time_grads(1, g_b, 2)
    add_cores(4)
    time_grads(0, g_b, 0)
    between[1].start()

    @pl.loop(0, F)
    def _(f):
        v = sd[f]
        left, right = columns(v)
        ys[f, 64:320, 0:256] = right
        ys[f, 64:320, 256:512] = v
        ys[f, 64:320, 512:768] = left

    add_cores(1)
    sd_up.wait()
    sd_dn.wait()

    @pl.when(r == 0)
    def _():
        sd_lo[...] = jnp.zeros_like(sd_lo)

    @pl.when(r == 15)
    def _():
        sd_hi[...] = jnp.zeros_like(sd_hi)

    @pl.loop(0, F)
    def _(f):
        for ref, at in ((sd_lo, 0), (sd_hi, 320)):
            v = ref[f]
            left, right = columns(v)
            ys[f, at : at + 64, 0:256] = right
            ys[f, at : at + 64, 256:512] = v
            ys[f, at : at + 64, 512:768] = left
    def input_grads(f, n, q):
        cat = jnp.concatenate(
            [
                ys[f : f + n, 64 * (2 - i) + HALF * q : 64 * (2 - i) + HALF * q + HALF, :].reshape(
                    n * HALF, 768
                )
                for i in range(3)
            ],
            axis=1,
        )
        total = dot(cat, wsT[...].reshape(2304, 256)) + past(cot, f, n, q).astype(F32)
        gin[f : f + n, half(q)] = total.astype(BF).reshape(n, HALF, N)

    def outputs(f, n, q):
        total = temporal(3, f, n, q) + past(lat, f, n, q).astype(F32)
        out[f : f + n, half(q)] = total.astype(BF).reshape(n, HALF, N)

    input_grads(0, 4, 0)
    input_grads(4, 4, 0)
    add_z(0, mb_t, 4)
    to_owner(4, 8, mb_t, rc_t, 0, 8)
    input_grads(0, 4, 1)
    input_grads(4, 4, 1)
    gin_store = pltpu.make_async_copy(gin, gin_hbm, load_sem.at[4])
    gin_store.start()
    add_z(2, mb_s, 0)
    to_owner(0, 3, mb_s, rc_s, 1, 0)
    for q in range(2):
        arrived_state(3, q)
        outputs(0, 4, q)
        outputs(4, 4, q)
    out_store = pltpu.make_async_copy(out, out_hbm, load_sem.at[5])
    out_store.start()
    add_z(3, mb_s, 3)
    to_owner(3, 6, mb_s, rc_s, 1, 0)
    add_z(4, mb_s, 6)
    to_owner(6, 9, mb_s, rc_s, 1, 0)
    add_z(1, mb_t, 0)
    to_owner(0, 4, mb_t, rc_t, 0, 8)
    own_sum(9, mb_s, rc_s, mc_s, 1, 0)
    own_sum(8, mb_t, rc_t, mc_t, 0, 8)
    for n in range(5):
        sent_z(n)
    finish(9, mb_s, rc_s, mc_s, 1, 0, gs_out)
    finish(8, mb_t, rc_t, mc_t, 0, 8, gt_out)
    gin_store.wait()
    out_store.wait()
def handed_on(*refs):
    sem = refs[-1]
    loads = [pltpu.make_async_copy(refs[k], refs[8 + k], sem.at[0, k]) for k in range(4)]
    stores = [pltpu.make_async_copy(refs[8 + k], refs[4 + k], sem.at[1, k]) for k in range(4)]
    for copy in loads:
        copy.start()
    for load, store in zip(loads, stores):
        load.wait()
        store.start()
    for copy in stores:
        copy.wait()


def shards(latents, cotangent, w_spatial, w_time):
    shape = latents.shape
    vmem = pl.BlockSpec(memory_space=pltpu.VMEM)
    hbm = pl.BlockSpec(memory_space=pl.ANY)
    V = pltpu.VMEM
    DMA = pltpu.SemaphoreType.DMA
    sizes = (4, 4, 3, 3, 3)
    scratch = [
        V((F, N, N), BF), V((F, N, N), BF), V((3, 768, N), BF), V((4, 512, N), BF),
        V((F, N, N), BF), V((F, N, N), BF),
        V((F, 384, 768), BF), V((F, 384, 768), BF),
        V((F, 64, N), BF), V((F, 64, N), BF), V((F, 64, N), BF), V((F, 64, N), BF),
        V((9, N, N), BF), V((10, N, N), BF), V((12, N, N), BF), V((16, N, N), BF),
        V((4, F, N, N), F32),
        V((9, N, N), BF), V((10, N, N), BF), V((12, N, N), BF), V((F, N, N), BF), V((F, N, N), BF),
        V((512, 2048), BF), V((3, 768, 256), BF), V((4, 512, 256), BF),
        *[V((2, 8, n, 16, N), BF) for n in sizes],
        *[V((8, n, 16, N), BF) for n in sizes],
        *[V((8, n, 16, N), BF) for n in sizes],
        *[V((8, n, 16, N), BF) for n in sizes],
        V((8, 16, N), BF), V((9, 16, N), BF),
        V((16, 16, N), BF), V((16, 16, N), BF),
        V((8, 16, N), BF), V((9, 16, N), BF),
        DMA((6,)), DMA((8,)), DMA((2, 8)), DMA((2, 8)), DMA((5, 2)),
        DMA((5, 8)), DMA((5, 8)), DMA((2, 9)), DMA((2, 16)), DMA((2, 16)), DMA((2, 9)),
    ]
    results = [
        jax.ShapeDtypeStruct((F, N, N), BF),
        jax.ShapeDtypeStruct((F, N, N), BF),
        jax.ShapeDtypeStruct((9, 16, N), F32),
        jax.ShapeDtypeStruct((8, 16, N), F32),
    ]
    held = pl.pallas_call(
        kernel,
        out_shape=results,
        in_specs=[hbm] * 4,
        out_specs=[hbm, hbm, vmem, vmem],
        scratch_shapes=scratch,
        compiler_params=pltpu.CompilerParams(
            collective_id=0, has_side_effects=True, vmem_limit_bytes=60 * 1024 * 1024
        ),
        cost_estimate=pl.CostEstimate(
            flops=51 * 2 * 2048 * N * N, bytes_accessed=7 * 1024 * 1024, transcendentals=4 * 2048 * N
        ),
    )(
        latents.reshape(F, N, N), cotangent.reshape(F, N, N),
        w_spatial.reshape(3, 768, N), w_time.reshape(4, 512, N),
    )
    out, gin, gs, gt = pl.pallas_call(
        handed_on,
        out_shape=results,
        in_specs=[hbm] * 4,
        out_specs=[hbm] * 4,
        scratch_shapes=[*[V(x.shape, x.dtype) for x in results], DMA((2, 4))],
        cost_estimate=pl.CostEstimate(flops=0, bytes_accessed=5 * 1024 * 1024, transcendentals=0),
    )(*held)
    spatial = jnp.swapaxes(gs, 1, 2)
    time = jnp.swapaxes(gt, 1, 2).reshape(4, 2, N, 16)
    return out.reshape(shape), gin.reshape(shape), spatial, time


def solution(mesh):
    in_specs = (P("tm", "rows", None, None), P("tm", "rows", None, None), P(), P())
    out_specs = (
        P("tm", "rows", None, None),
        P("tm", "rows", None, None),
        P(None, None, "rows"),
        P(None, None, None, "rows"),
    )
    return jax.shard_map(shards, mesh=mesh, in_specs=in_specs, out_specs=out_specs, check_vma=False)
```

```python
import math

import jax
import jax.numpy as jnp
from jax import lax
from jax.experimental import pallas as pl
from jax.experimental.pallas import tpu as pltpu
from jax.sharding import PartitionSpec as P

MESH = pl.DeviceIdType.MESH
F = 8
N = 256
HALF = 128
BF = jnp.bfloat16
F32 = jnp.float32


def dot(a, b):
    return lax.dot_general(a, b, (((1,), (0,)), ((), ())), preferred_element_type=F32)


def columns(v):
    wide = v.astype(F32)
    n = wide.shape[0]
    col = lax.rem(lax.broadcasted_iota(jnp.int32, wide.shape, 0), 64)
    left = jnp.where(col == 0, 0.0, pltpu.roll(wide, 1, 0)).astype(BF)
    right = jnp.where(col == 63, 0.0, pltpu.roll(wide, n - 1, 0)).astype(BF)
    return left, right


def kernel(
    lat_in, cot_in, ws_in, wt_in,
    out_hbm, gin_hbm, gs_out, gt_out,
    lat, cot, ws, wt, out, gin,
    xs, ys, lat_lo, lat_hi, sd_lo, sd_hi,
    s0, s1, s2, s3, slope, d0, d1, d2, d3h, sd, dT, wsT, wtT,
    g_a, g_b, g_x, g_y, g_z,
    ra_a, ra_b, ra_x, ra_y, ra_z,
    ma_a, ma_b, ma_x, ma_y, ma_z,
    rp_a, rp_b, rp_x, rp_y, rp_z,
    rm_a, rm_b, rm_x, rm_y, rm_z,
    sp_a, sp_b, sp_x, sp_y, sp_z,
    sm_a, sm_b, sm_x, sm_y, sm_z,
    mb_t, mb_s, rc_t, rc_s, mc_t, mc_s,
    load_sem, row_sem, tm_send, tm_recv, a_sem, b_send, b_recv, c_send, c_recv, h_send, h_recv,
):
    t = lax.axis_index("tm")
    r = lax.axis_index("rows")
    z = r // 2
    c = lax.rem(r, 2)
    tm_next = lax.rem(t + 1, 16)
    tm_prev = lax.rem(t + 15, 16)
    r_next = lax.rem(r + 1, 16)
    r_prev = lax.rem(r + 15, 16)
    sibling = r + 1 - 2 * c
    far = lax.rem(r + 15 + 2 * c, 16)
    states = (s0, s1, s2, s3)
    deltas = (d0, d1, d2, d3h)
    factor = 1.0 / math.sqrt(524288.0)
    barrier = pltpu.get_barrier_semaphore()
    for k in (1, 15, 2, 14, 3, 13, 4, 12, 5, 11, 6, 10, 7, 9, 8):
        pl.semaphore_signal(barrier, inc=1, device_id=(lax.rem(t + k, 16), r), device_id_type=MESH)
    for k in (2, 14):
        pl.semaphore_signal(
            barrier, inc=1, device_id=(t, lax.rem(r + k, 16)), device_id_type=MESH
        )
    pl.semaphore_signal(barrier, inc=1, device_id=(t, sibling), device_id_type=MESH)
    pl.semaphore_signal(barrier, inc=1, device_id=(t, far), device_id_type=MESH)

    loads = [
        pltpu.make_async_copy(src, dst, load_sem.at[k])
        for k, (src, dst) in enumerate(((lat_in, lat), (ws_in, ws), (wt_in, wt), (cot_in, cot)))
    ]
    for copy in loads:
        copy.start()
    pl.semaphore_wait(barrier, 19)

    def remote(src, dst, send, recv, device):
        return pltpu.make_async_remote_copy(
            src_ref=src, dst_ref=dst, send_sem=send, recv_sem=recv, device_id=device,
            device_id_type=MESH,
        )
    lat_up = remote(lat_in.at[:, 192:256], lat_lo, row_sem.at[0], row_sem.at[1], (t, r_next))
    lat_dn = remote(lat_in.at[:, 0:64], lat_hi, row_sem.at[2], row_sem.at[3], (t, r_prev))
    lat_up.start()
    lat_dn.start()

    def half(q):
        return slice(HALF * q, HALF * q + HALF)

    state_up = [
        [
            remote(
                states[k].at[8 : 8 + 2**k, half(q)], states[k].at[0 : 2**k, half(q)],
                tm_send.at[q, k], tm_recv.at[q, k], (tm_next, r),
            )
            for k in range(4)
        ]
        for q in range(2)
    ]
    delta_dn = [
        [
            remote(
                deltas[k].at[0 : 2**k, half(q)], deltas[k].at[8 : 8 + 2**k, half(q)],
                tm_send.at[q, 4 + k], tm_recv.at[q, 4 + k], (tm_prev, r),
            )
            for k in range(3)
        ]
        + [
            remote(
                cot_in.at[:, half(q)], d3h.at[:, half(q)], tm_send.at[q, 7], tm_recv.at[q, 7],
                (tm_prev, r),
            )
        ]
        for q in range(2)
    ]
    delta_dn[0][3].start()
    delta_dn[1][3].start()

    loads[0].wait()

    @pl.loop(0, F)
    def _(f):
        v = lat[f]
        left, right = columns(v)
        xs[f, 64:320, 0:256] = left
        xs[f, 64:320, 256:512] = v
        xs[f, 64:320, 512:768] = right

    loads[1].wait()
    lat_up.wait()
    lat_dn.wait()

    @pl.when(r == 0)
    def _():
        lat_lo[...] = jnp.zeros_like(lat_lo)

    @pl.when(r == 15)
    def _():
        lat_hi[...] = jnp.zeros_like(lat_hi)

    @pl.loop(0, F)
    def _(f):
        for ref, at in ((lat_lo, 0), (lat_hi, 320)):
            v = ref[f]
            left, right = columns(v)
            xs[f, at : at + 64, 0:256] = left
            xs[f, at : at + 64, 256:512] = v
            xs[f, at : at + 64, 512:768] = right

    def activate(k, f, n, q, v):
        sigma = 0.5 + 0.5 * jnp.tanh(0.5 * v)
        state = v * sigma
        states[k][2**k + f : 2**k + f + n, half(q)] = state.astype(BF).reshape(n, HALF, N)
        slope[k, f : f + n, half(q)] = (sigma + state * (1.0 - sigma)).reshape(n, HALF, N)

    def conv(f, n, q):
        cat = jnp.concatenate(
            [
                xs[f : f + n, 64 * i + HALF * q : 64 * i + HALF * q + HALF, :].reshape(n * HALF, 768)
                for i in range(3)
            ],
            axis=1,
        )
        activate(0, f, n, q, dot(cat, ws[...].reshape(2304, 256)))

    def past(ref, at, n, q):
        return ref[at : at + n, half(q)].reshape(n * HALF, N)

    def temporal(k, f, n, q):
        cat = jnp.concatenate(
            [past(states[k], f + 2**k, n, q), past(states[k], f, n, q)], axis=1
        )
        return dot(cat, wt[k])

    def forward(k, f, n, q):
        activate(k + 1, f, n, q, temporal(k, f, n, q))

    def arrived_state(k, q):
        state_up[q][k].wait()

        @pl.when(t == 0)
        def _():
            states[k][0 : 2**k, half(q)] = jnp.zeros((2**k, HALF, N), BF)
    for q in range(2):
        conv(4, 4, q)
        state_up[q][0].start()
        conv(0, 4, q)
        if q == 0:
            loads[2].wait()
        forward(0, 4, 4, q)
        state_up[q][1].start()
        forward(0, 1, 3, q)
        forward(1, 4, 4, q)
        state_up[q][2].start()
        forward(1, 3, 1, q)
    for i in range(3):
        for j in range(3):
            wsT[i, 256 * j : 256 * j + 256, :] = ws[i, 256 * j : 256 * j + 256, :].T

    @pl.loop(0, 4)
    def _(k):
        wtT[k, 0:256, :] = wt[k, 0:256, :].T
        wtT[k, 256:512, :] = wt[k, 256:512, :].T

    loads[3].wait()

    def back(k, f, n, q):
        source = cot if k == 3 else deltas[k]
        later = past(d3h, f, n, q) if k == 3 else past(deltas[k], f + 2**k, n, q)
        total = dot(jnp.concatenate([past(source, f, n, q), later], axis=1), wtT[k])
        value = (total * past(slope.at[k], f, n, q)).astype(BF)
        target = sd if k == 0 else deltas[k - 1]
        target[f : f + n, half(q)] = value.reshape(n, HALF, N)

    def arrived_delta(k, q):
        delta_dn[q][k].wait()
        at = 0 if k == 3 else 8

        @pl.when(t == 15)
        def _():
            deltas[k][at : at + 2**k, half(q)] = jnp.zeros((2**k, HALF, N), BF)

    for q in range(2):
        arrived_state(0, q)
        forward(0, 0, 1, q)
        arrived_state(1, q)
        forward(1, 0, 3, q)
        forward(2, 4, 4, q)
        arrived_state(2, q)
        forward(2, 0, 4, q)
        state_up[q][3].start()
        arrived_delta(3, q)
        back(3, 0, 4, q)
        delta_dn[q][2].start()
        back(3, 4, 4, q)
        back(2, 0, 4, q)
        delta_dn[q][1].start()
        back(1, 0, 2, q)
        delta_dn[q][0].start()

    def put(ref, tap, value):
        for part in range(16):
            ref[part % 2, part // 2, tap] = value[16 * part : 16 * part + 16].astype(BF)

    def time_grads(k, ref, tap):
        d = 2**k
        for f in range(F):
            src = cot if k == 3 else deltas[k]
            dT[0:256, 256 * f : 256 * f + 256] = src[f].T
            other = d3h[f] if k == 3 else deltas[k][f + d]
            dT[256:512, 256 * f : 256 * f + 256] = other.T
        both = dot(dT[...], states[k][d : d + F].reshape(2048, N))
        put(ref, tap, both[0:256])
        put(ref, tap + 1, both[256:512])

    groups = [
        (g_a, ra_a, ma_a, rp_a, rm_a, sp_a, sm_a),
        (g_b, ra_b, ma_b, rp_b, rm_b, sp_b, sm_b),
        (g_x, ra_x, ma_x, rp_x, rm_x, sp_x, sm_x),
        (g_y, ra_y, ma_y, rp_y, rm_y, sp_y, sm_y),
        (g_z, ra_z, ma_z, rp_z, rm_z, sp_z, sm_z),
    ]
    between = [
        remote(group[0].at[1 - c], group[1], a_sem.at[n, 0], a_sem.at[n, 1], (t, sibling))
        for n, group in enumerate(groups)
    ]

    def upward(n, step):
        _, _, ma, rp, _, sp, _ = groups[n]
        source = ma.at[lax.rem(z + 4, 8)] if step == 0 else sp.at[step - 1]
        return remote(
            source, rp.at[step], b_send.at[n, step], b_recv.at[n, step],
            (t, lax.rem(r + 2, 16)),
        )

    def downward(n, step):
        _, _, ma, _, rm, _, sm = groups[n]
        source = ma.at[lax.rem(z + 5, 8)] if step == 0 else sm.at[step - 1]
        return remote(
            source, rm.at[step], b_send.at[n, 4 + step], b_recv.at[n, 4 + step],
            (t, lax.rem(r + 14, 16)),
        )

    def add_cores(n):
        g, ra, ma = groups[n][:3]
        between[n].wait()

        @pl.loop(0, 8)
        def _(p):
            ma[p] = (g[c, p].astype(F32) + ra[p].astype(F32)).astype(BF)

        upward(n, 0).start()
        downward(n, 0).start()

    def pass_on(n, step):
        _, _, ma, rp, rm, sp, sm = groups[n]
        upward(n, step - 1).wait_recv()
        sp[step - 1] = (ma[lax.rem(z + 4 - step, 8)].astype(F32) + rp[step - 1].astype(F32)).astype(BF)
        upward(n, step).start()
        if step < 3:
            downward(n, step - 1).wait_recv()
            sm[step - 1] = (
                ma[lax.rem(z + 5 + step, 8)].astype(F32) + rm[step - 1].astype(F32)
            ).astype(BF)
            downward(n, step).start()

    def add_z(n, mb, at):
        _, _, ma, rp, rm, _, _ = groups[n]
        taps = ma.shape[1]
        upward(n, 3).wait_recv()
        downward(n, 2).wait_recv()
        total = ma[z].astype(F32) + rp[3].astype(F32) + rm[2].astype(F32)
        mb[at : at + taps] = total.astype(BF)

    def sent_z(n):
        for step in range(4):
            upward(n, step).wait_send()
        for step in range(3):
            downward(n, step).wait_send()

    def to_owner(low, high, mb, rc, group, first):
        for k in range(low, high):
            owner = first + k

            @pl.when(t != owner)
            def _():
                remote(
                    mb.at[k], rc.at[t], c_send.at[group, k], c_recv.at[group, t], (owner, r)
                ).start()

    def own_sum(taps, mb, rc, mc, group, first):
        mine = t - first

        @pl.when((t >= first) & (t < first + taps))
        def _():
            rc[t] = mb[mine]
            for k in range(1, 16):
                source = lax.rem(t + k, 16)
                remote(
                    rc.at[source], rc.at[source], c_send.at[group, 0], c_recv.at[group, source],
                    (source, r),
                ).wait_recv()
            total = rc[0].astype(F32)
            for p in range(1, 16):
                total = total + rc[p].astype(F32)
            mc[mine] = total.astype(BF)
            for k in range(1, 16):
                remote(
                    mc.at[mine], mc.at[mine], h_send.at[group, k], h_recv.at[group, mine],
                    (lax.rem(t + k, 16), r),
                ).start()

    def finish(taps, mb, rc, mc, group, first, target):
        mine = t - first
        for k in range(taps):
            owner = first + k

            @pl.when(t != owner)
            def _():
                remote(
                    mb.at[k], rc.at[t], c_send.at[group, k], c_recv.at[group, t], (owner, r)
                ).wait_send()
                remote(
                    mc.at[k], mc.at[k], h_send.at[group, 0], h_recv.at[group, k], (owner, r)
                ).wait_recv()

        target[...] = mc[...].astype(F32) * factor

        @pl.when((t >= first) & (t < first + taps))
        def _():
            for k in range(1, 16):
                remote(
                    mc.at[mine], mc.at[mine], h_send.at[group, k], h_recv.at[group, mine],
                    (lax.rem(t + k, 16), r),
                ).wait_send()
    time_grads(3, g_a, 2)
    arrived_delta(2, 0)
    back(2, 4, 4, 0)
    back(1, 2, 2, 0)
    arrived_delta(1, 0)
    back(1, 4, 4, 0)
    back(0, 0, 4, 0)
    arrived_delta(0, 0)
    back(0, 4, 4, 0)
    sd_dn = remote(sd.at[:, 0:64], sd_hi, row_sem.at[6], row_sem.at[7], (t, r_prev))
    sd_dn.start()
    arrived_delta(2, 1)
    back(2, 4, 4, 1)
    back(1, 2, 2, 1)
    time_grads(2, g_a, 0)
    between[0].start()
    arrived_delta(1, 1)
    back(1, 4, 4, 1)
    back(0, 0, 4, 1)
    time_grads(1, g_b, 2)
    add_cores(0)
    arrived_delta(0, 1)
    back(0, 4, 4, 1)
    sd_up = remote(sd.at[:, 192:256], sd_lo, row_sem.at[4], row_sem.at[5], (t, r_next))
    sd_up.start()

    def spatial_grads(i, ref):
        rows = xs[:, 64 * i : 64 * i + 256, :].reshape(2048, 768)
        total = dot(dT[0:256, :], rows)
        for j in range(3):
            put(ref, j, total[:, 256 * j : 256 * j + 256])

    time_grads(0, g_b, 0)
    between[1].start()
    pass_on(0, 1)
    for f in range(F):
        dT[0:256, 256 * f : 256 * f + 256] = sd[f].T
    spatial_grads(0, g_x)
    between[2].start()
    pass_on(0, 2)
    add_cores(1)
    spatial_grads(1, g_y)
    between[3].start()
    add_cores(2)
    pass_on(0, 3)
    pass_on(1, 1)
    spatial_grads(2, g_z)
    between[4].start()
    add_cores(3)
    pass_on(1, 2)
    pass_on(2, 1)
    add_z(0, mb_t, 4)
    to_owner(4, 8, mb_t, rc_t, 0, 8)
    @pl.loop(0, F)
    def _(f):
        v = sd[f]
        left, right = columns(v)
        ys[f, 64:320, 0:256] = right
        ys[f, 64:320, 256:512] = v
        ys[f, 64:320, 512:768] = left

    add_cores(4)
    pass_on(1, 3)
    pass_on(2, 2)
    pass_on(3, 1)
    sd_up.wait()
    sd_dn.wait()

    @pl.when(r == 0)
    def _():
        sd_lo[...] = jnp.zeros_like(sd_lo)

    @pl.when(r == 15)
    def _():
        sd_hi[...] = jnp.zeros_like(sd_hi)

    @pl.loop(0, F)
    def _(f):
        for ref, at in ((sd_lo, 0), (sd_hi, 320)):
            v = ref[f]
            left, right = columns(v)
            ys[f, at : at + 64, 0:256] = right
            ys[f, at : at + 64, 256:512] = v
            ys[f, at : at + 64, 512:768] = left

    pass_on(2, 3)
    pass_on(3, 2)
    pass_on(4, 1)
    add_z(1, mb_t, 0)
    to_owner(0, 4, mb_t, rc_t, 0, 8)
    def input_grads(f, n, q):
        cat = jnp.concatenate(
            [
                ys[f : f + n, 64 * (2 - i) + HALF * q : 64 * (2 - i) + HALF * q + HALF, :].reshape(
                    n * HALF, 768
                )
                for i in range(3)
            ],
            axis=1,
        )
        total = dot(cat, wsT[...].reshape(2304, 256)) + past(cot, f, n, q).astype(F32)
        gin[f : f + n, half(q)] = total.astype(BF).reshape(n, HALF, N)

    def outputs(f, n, q):
        total = temporal(3, f, n, q) + past(lat, f, n, q).astype(F32)
        out[f : f + n, half(q)] = total.astype(BF).reshape(n, HALF, N)

    input_grads(0, 4, 0)
    pass_on(3, 3)
    pass_on(4, 2)
    add_z(2, mb_s, 0)
    to_owner(0, 3, mb_s, rc_s, 1, 0)
    input_grads(4, 4, 0)
    pass_on(4, 3)
    add_z(3, mb_s, 3)
    to_owner(3, 6, mb_s, rc_s, 1, 0)
    input_grads(0, 4, 1)
    add_z(4, mb_s, 6)
    to_owner(6, 9, mb_s, rc_s, 1, 0)
    own_sum(8, mb_t, rc_t, mc_t, 0, 8)
    input_grads(4, 4, 1)
    gin_store = pltpu.make_async_copy(gin, gin_hbm, load_sem.at[4])
    gin_store.start()
    own_sum(9, mb_s, rc_s, mc_s, 1, 0)
    for q in range(2):
        arrived_state(3, q)
        outputs(0, 4, q)
        outputs(4, 4, q)
    out_store = pltpu.make_async_copy(out, out_hbm, load_sem.at[5])
    out_store.start()
    for n in range(5):
        sent_z(n)
    finish(8, mb_t, rc_t, mc_t, 0, 8, gt_out)
    finish(9, mb_s, rc_s, mc_s, 1, 0, gs_out)
    gin_store.wait()
    out_store.wait()
def handed_on(*refs):
    sem = refs[-1]
    loads = [pltpu.make_async_copy(refs[k], refs[8 + k], sem.at[0, k]) for k in range(4)]
    stores = [pltpu.make_async_copy(refs[8 + k], refs[4 + k], sem.at[1, k]) for k in range(4)]
    for copy in loads:
        copy.start()
    for load, store in zip(loads, stores):
        load.wait()
        store.start()
    for copy in stores:
        copy.wait()


def shards(latents, cotangent, w_spatial, w_time):
    shape = latents.shape
    vmem = pl.BlockSpec(memory_space=pltpu.VMEM)
    hbm = pl.BlockSpec(memory_space=pl.ANY)
    V = pltpu.VMEM
    DMA = pltpu.SemaphoreType.DMA
    sizes = (4, 4, 3, 3, 3)
    scratch = [
        V((F, N, N), BF), V((F, N, N), BF), V((3, 768, N), BF), V((4, 512, N), BF),
        V((F, N, N), BF), V((F, N, N), BF),
        V((F, 384, 768), BF), V((F, 384, 768), BF),
        V((F, 64, N), BF), V((F, 64, N), BF), V((F, 64, N), BF), V((F, 64, N), BF),
        V((9, N, N), BF), V((10, N, N), BF), V((12, N, N), BF), V((16, N, N), BF),
        V((4, F, N, N), F32),
        V((9, N, N), BF), V((10, N, N), BF), V((12, N, N), BF), V((F, N, N), BF), V((F, N, N), BF),
        V((512, 2048), BF), V((3, 768, 256), BF), V((4, 512, 256), BF),
        *[V((2, 8, n, 16, N), BF) for n in sizes],
        *[V((8, n, 16, N), BF) for n in sizes],
        *[V((8, n, 16, N), BF) for n in sizes],
        *[V((4, n, 16, N), BF) for n in sizes],
        *[V((3, n, 16, N), BF) for n in sizes],
        *[V((3, n, 16, N), BF) for n in sizes],
        *[V((2, n, 16, N), BF) for n in sizes],
        V((8, 16, N), BF), V((9, 16, N), BF),
        V((16, 16, N), BF), V((16, 16, N), BF),
        V((8, 16, N), BF), V((9, 16, N), BF),
        DMA((6,)), DMA((8,)), DMA((2, 8)), DMA((2, 8)), DMA((5, 2)),
        DMA((5, 8)), DMA((5, 8)), DMA((2, 9)), DMA((2, 16)), DMA((2, 16)), DMA((2, 9)),
    ]
    results = [
        jax.ShapeDtypeStruct((F, N, N), BF),
        jax.ShapeDtypeStruct((F, N, N), BF),
        jax.ShapeDtypeStruct((9, 16, N), F32),
        jax.ShapeDtypeStruct((8, 16, N), F32),
    ]
    held = pl.pallas_call(
        kernel,
        out_shape=results,
        in_specs=[hbm] * 4,
        out_specs=[hbm, hbm, vmem, vmem],
        scratch_shapes=scratch,
        compiler_params=pltpu.CompilerParams(
            collective_id=0, has_side_effects=True, vmem_limit_bytes=60 * 1024 * 1024
        ),
        cost_estimate=pl.CostEstimate(
            flops=51 * 2 * 2048 * N * N, bytes_accessed=7 * 1024 * 1024, transcendentals=4 * 2048 * N
        ),
    )(
        latents.reshape(F, N, N), cotangent.reshape(F, N, N),
        w_spatial.reshape(3, 768, N), w_time.reshape(4, 512, N),
    )
    out, gin, gs, gt = pl.pallas_call(
        handed_on,
        out_shape=results,
        in_specs=[hbm] * 4,
        out_specs=[hbm] * 4,
        scratch_shapes=[*[V(x.shape, x.dtype) for x in results], DMA((2, 4))],
        cost_estimate=pl.CostEstimate(flops=0, bytes_accessed=5 * 1024 * 1024, transcendentals=0),
    )(*held)
    spatial = jnp.swapaxes(gs, 1, 2)
    time = jnp.swapaxes(gt, 1, 2).reshape(4, 2, N, 16)
    return out.reshape(shape), gin.reshape(shape), spatial, time


def solution(mesh):
    in_specs = (P("tm", "rows", None, None), P("tm", "rows", None, None), P(), P())
    out_specs = (
        P("tm", "rows", None, None),
        P("tm", "rows", None, None),
        P(None, None, "rows"),
        P(None, None, None, "rows"),
    )
    return jax.shard_map(shards, mesh=mesh, in_specs=in_specs, out_specs=out_specs, check_vma=False)
```

```python
import math

import jax
import jax.numpy as jnp
from jax import lax
from jax.experimental import pallas as pl
from jax.experimental.pallas import tpu as pltpu
from jax.sharding import PartitionSpec as P

MESH = pl.DeviceIdType.MESH
F = 8
N = 256
HALF = 128
BF = jnp.bfloat16
F32 = jnp.float32


def dot(a, b):
    return lax.dot_general(a, b, (((1,), (0,)), ((), ())), preferred_element_type=F32)


def columns(v):
    wide = v.astype(F32)
    n = wide.shape[0]
    col = lax.rem(lax.broadcasted_iota(jnp.int32, wide.shape, 0), 64)
    left = jnp.where(col == 0, 0.0, pltpu.roll(wide, 1, 0)).astype(BF)
    right = jnp.where(col == 63, 0.0, pltpu.roll(wide, n - 1, 0)).astype(BF)
    return left, right


def kernel(
    lat_in, cot_in, ws_in, wt_in,
    out_hbm, gin_hbm, gs_out, gt_out,
    lat, cot, ws, wt, out, gin,
    xs, ys, lat_lo, lat_hi, sd_lo, sd_hi,
    s0, s1, s2, s3, slope, d0, d1, d2, d3h, sd, dT, wsT, wtT,
    g_0, g_1, g_2, g_3, g_x, g_y, g_z,
    ra_0, ra_1, ra_2, ra_3, ra_x, ra_y, ra_z,
    ma_0, ma_1, ma_2, ma_3, ma_x, ma_y, ma_z,
    rb_0, rb_1, rb_2, rb_3, rb_x, rb_y, rb_z,
    mb_t, mb_s, rc_t, rc_s, mc_t, mc_s,
    load_sem, row_sem, tm_send, tm_recv, a_sem, b_send, b_recv, c_send, c_recv, h_send, h_recv,
):
    t = lax.axis_index("tm")
    r = lax.axis_index("rows")
    z = r // 2
    c = lax.rem(r, 2)
    tm_next = lax.rem(t + 1, 16)
    tm_prev = lax.rem(t + 15, 16)
    r_next = lax.rem(r + 1, 16)
    r_prev = lax.rem(r + 15, 16)
    sibling = r + 1 - 2 * c
    far = lax.rem(r + 15 + 2 * c, 16)
    states = (s0, s1, s2, s3)
    deltas = (d0, d1, d2, d3h)
    factor = 1.0 / math.sqrt(524288.0)
    barrier = pltpu.get_barrier_semaphore()
    for k in (1, 15, 2, 14, 3, 13, 4, 12, 5, 11, 6, 10, 7, 9, 8):
        pl.semaphore_signal(barrier, inc=1, device_id=(lax.rem(t + k, 16), r), device_id_type=MESH)
    for k in range(1, 8):
        pl.semaphore_signal(
            barrier, inc=1, device_id=(t, lax.rem(r + 2 * k, 16)), device_id_type=MESH
        )
    pl.semaphore_signal(barrier, inc=1, device_id=(t, sibling), device_id_type=MESH)
    pl.semaphore_signal(barrier, inc=1, device_id=(t, far), device_id_type=MESH)

    loads = [
        pltpu.make_async_copy(src, dst, load_sem.at[k])
        for k, (src, dst) in enumerate(((lat_in, lat), (ws_in, ws), (wt_in, wt), (cot_in, cot)))
    ]
    for copy in loads:
        copy.start()
    pl.semaphore_wait(barrier, 24)

    def remote(src, dst, send, recv, device):
        return pltpu.make_async_remote_copy(
            src_ref=src, dst_ref=dst, send_sem=send, recv_sem=recv, device_id=device,
            device_id_type=MESH,
        )
    lat_up = remote(lat_in.at[:, 192:256], lat_lo, row_sem.at[0], row_sem.at[1], (t, r_next))
    lat_dn = remote(lat_in.at[:, 0:64], lat_hi, row_sem.at[2], row_sem.at[3], (t, r_prev))
    lat_up.start()
    lat_dn.start()

    def half(q):
        return slice(HALF * q, HALF * q + HALF)

    state_up = [
        [
            remote(
                states[k].at[8 : 8 + 2**k, half(q)], states[k].at[0 : 2**k, half(q)],
                tm_send.at[q, k], tm_recv.at[q, k], (tm_next, r),
            )
            for k in range(4)
        ]
        for q in range(2)
    ]
    delta_dn = [
        [
            remote(
                deltas[k].at[0 : 2**k, half(q)], deltas[k].at[8 : 8 + 2**k, half(q)],
                tm_send.at[q, 4 + k], tm_recv.at[q, 4 + k], (tm_prev, r),
            )
            for k in range(3)
        ]
        + [
            remote(
                cot_in.at[:, half(q)], d3h.at[:, half(q)], tm_send.at[q, 7], tm_recv.at[q, 7],
                (tm_prev, r),
            )
        ]
        for q in range(2)
    ]
    delta_dn[0][3].start()
    delta_dn[1][3].start()

    loads[0].wait()

    @pl.loop(0, F)
    def _(f):
        v = lat[f]
        left, right = columns(v)
        xs[f, 64:320, 0:256] = left
        xs[f, 64:320, 256:512] = v
        xs[f, 64:320, 512:768] = right

    loads[1].wait()
    lat_up.wait()
    lat_dn.wait()

    @pl.when(r == 0)
    def _():
        lat_lo[...] = jnp.zeros_like(lat_lo)

    @pl.when(r == 15)
    def _():
        lat_hi[...] = jnp.zeros_like(lat_hi)

    @pl.loop(0, F)
    def _(f):
        for ref, at in ((lat_lo, 0), (lat_hi, 320)):
            v = ref[f]
            left, right = columns(v)
            xs[f, at : at + 64, 0:256] = left
            xs[f, at : at + 64, 256:512] = v
            xs[f, at : at + 64, 512:768] = right

    def activate(k, f, n, q, v):
        sigma = 0.5 + 0.5 * jnp.tanh(0.5 * v)
        state = v * sigma
        states[k][2**k + f : 2**k + f + n, half(q)] = state.astype(BF).reshape(n, HALF, N)
        slope[k, f : f + n, half(q)] = (sigma + state * (1.0 - sigma)).reshape(n, HALF, N)

    def conv(f, n, q):
        cat = jnp.concatenate(
            [
                xs[f : f + n, 64 * i + HALF * q : 64 * i + HALF * q + HALF, :].reshape(n * HALF, 768)
                for i in range(3)
            ],
            axis=1,
        )
        activate(0, f, n, q, dot(cat, ws[...].reshape(2304, 256)))

    def past(ref, at, n, q):
        return ref[at : at + n, half(q)].reshape(n * HALF, N)

    def temporal(k, f, n, q):
        cat = jnp.concatenate(
            [past(states[k], f + 2**k, n, q), past(states[k], f, n, q)], axis=1
        )
        return dot(cat, wt[k])

    def forward(k, f, n, q):
        activate(k + 1, f, n, q, temporal(k, f, n, q))

    def arrived_state(k, q):
        state_up[q][k].wait()

        @pl.when(t == 0)
        def _():
            states[k][0 : 2**k, half(q)] = jnp.zeros((2**k, HALF, N), BF)
    for q in range(2):
        conv(4, 4, q)
        state_up[q][0].start()
        conv(0, 4, q)
        if q == 0:
            loads[2].wait()
        forward(0, 4, 4, q)
        state_up[q][1].start()
        forward(0, 1, 3, q)
        forward(1, 4, 4, q)
        state_up[q][2].start()
        forward(1, 3, 1, q)
    for i in range(3):
        for j in range(3):
            wsT[i, 256 * j : 256 * j + 256, :] = ws[i, 256 * j : 256 * j + 256, :].T

    @pl.loop(0, 4)
    def _(k):
        wtT[k, 0:256, :] = wt[k, 0:256, :].T
        wtT[k, 256:512, :] = wt[k, 256:512, :].T

    loads[3].wait()

    def back(k, f, n, q):
        source = cot if k == 3 else deltas[k]
        later = past(d3h, f, n, q) if k == 3 else past(deltas[k], f + 2**k, n, q)
        total = dot(jnp.concatenate([past(source, f, n, q), later], axis=1), wtT[k])
        value = (total * past(slope.at[k], f, n, q)).astype(BF)
        target = sd if k == 0 else deltas[k - 1]
        target[f : f + n, half(q)] = value.reshape(n, HALF, N)

    def arrived_delta(k, q):
        delta_dn[q][k].wait()
        at = 0 if k == 3 else 8

        @pl.when(t == 15)
        def _():
            deltas[k][at : at + 2**k, half(q)] = jnp.zeros((2**k, HALF, N), BF)

    for q in range(2):
        arrived_state(0, q)
        forward(0, 0, 1, q)
        arrived_state(1, q)
        forward(1, 0, 3, q)
        forward(2, 4, 4, q)
        arrived_state(2, q)
        forward(2, 0, 4, q)
        state_up[q][3].start()
        arrived_delta(3, q)
        back(3, 0, 4, q)
        delta_dn[q][2].start()
        back(3, 4, 4, q)
        back(2, 0, 4, q)
        delta_dn[q][1].start()
        back(1, 0, 2, q)
        delta_dn[q][0].start()

    def put(ref, tap, value):
        for part in range(16):
            ref[part % 2, part // 2, tap] = value[16 * part : 16 * part + 16].astype(BF)

    def time_grads(k, ref, tap):
        d = 2**k
        for f in range(F):
            src = cot if k == 3 else deltas[k]
            dT[0:256, 256 * f : 256 * f + 256] = src[f].T
            other = d3h[f] if k == 3 else deltas[k][f + d]
            dT[256:512, 256 * f : 256 * f + 256] = other.T
        both = dot(dT[...], states[k][d : d + F].reshape(2048, N))
        put(ref, tap, both[0:256])
        put(ref, tap + 1, both[256:512])

    groups = [
        (g_0, ra_0, ma_0, rb_0),
        (g_1, ra_1, ma_1, rb_1),
        (g_2, ra_2, ma_2, rb_2),
        (g_3, ra_3, ma_3, rb_3),
        (g_x, ra_x, ma_x, rb_x),
        (g_y, ra_y, ma_y, rb_y),
        (g_z, ra_z, ma_z, rb_z),
    ]
    between = [
        remote(g.at[1 - c], ra, a_sem.at[n, 0], a_sem.at[n, 1], (t, sibling))
        for n, (g, ra, _, _) in enumerate(groups)
    ]

    def z_copies(n):
        _, _, ma, rb = groups[n]
        return [
            remote(
                ma.at[lax.rem(z + k, 8)], rb.at[z], b_send.at[n, k], b_recv.at[n, z],
                (t, lax.rem(r + 2 * k, 16)),
            )
            for k in (4, 3, 5, 2, 6, 1, 7)
        ]

    def add_cores(n):
        g, ra, ma, rb = groups[n]
        between[n].wait()

        @pl.loop(0, 8)
        def _(p):
            ma[p] = (g[c, p].astype(F32) + ra[p].astype(F32)).astype(BF)

        for copy in z_copies(n):
            copy.start()
        rb[z] = ma[z]

    def add_z(n, mb, at):
        taps = groups[n][0].shape[2]
        rb = groups[n][3]
        for k in range(1, 8):
            source = lax.rem(z + 8 - k, 8)
            remote(
                rb.at[source], rb.at[source], b_send.at[n, k], b_recv.at[n, source],
                (t, lax.rem(r + 16 - 2 * k, 16)),
            ).wait_recv()
        total = rb[0].astype(F32)
        for p in range(1, 8):
            total = total + rb[p].astype(F32)
        mb[at : at + taps] = total.astype(BF)

    def sent_z(n):
        for copy in z_copies(n):
            copy.wait_send()

    def to_owner(low, high, mb, rc, group, first):
        for k in range(low, high):
            owner = first + k

            @pl.when(t != owner)
            def _():
                remote(
                    mb.at[k], rc.at[t], c_send.at[group, k], c_recv.at[group, t], (owner, r)
                ).start()

    def own_sum(taps, mb, rc, mc, group, first):
        mine = t - first

        @pl.when((t >= first) & (t < first + taps))
        def _():
            rc[t] = mb[mine]
            for k in range(1, 16):
                source = lax.rem(t + k, 16)
                remote(
                    rc.at[source], rc.at[source], c_send.at[group, 0], c_recv.at[group, source],
                    (source, r),
                ).wait_recv()
            total = rc[0].astype(F32)
            for p in range(1, 16):
                total = total + rc[p].astype(F32)
            mc[mine] = total.astype(BF)
            for k in range(1, 16):
                remote(
                    mc.at[mine], mc.at[mine], h_send.at[group, k], h_recv.at[group, mine],
                    (lax.rem(t + k, 16), r),
                ).start()

    def finish(taps, mb, rc, mc, group, first, target):
        mine = t - first
        for k in range(taps):
            owner = first + k

            @pl.when(t != owner)
            def _():
                remote(
                    mb.at[k], rc.at[t], c_send.at[group, k], c_recv.at[group, t], (owner, r)
                ).wait_send()
                remote(
                    mc.at[k], mc.at[k], h_send.at[group, 0], h_recv.at[group, k], (owner, r)
                ).wait_recv()

        target[...] = mc[...].astype(F32) * factor

        @pl.when((t >= first) & (t < first + taps))
        def _():
            for k in range(1, 16):
                remote(
                    mc.at[mine], mc.at[mine], h_send.at[group, k], h_recv.at[group, mine],
                    (lax.rem(t + k, 16), r),
                ).wait_send()
    time_grads(3, g_3, 0)
    between[3].start()
    arrived_delta(2, 0)
    back(2, 4, 4, 0)
    back(1, 2, 2, 0)
    arrived_delta(1, 0)
    back(1, 4, 4, 0)
    back(0, 0, 4, 0)
    add_cores(3)
    arrived_delta(0, 0)
    back(0, 4, 4, 0)
    sd_dn = remote(sd.at[:, 0:64], sd_hi, row_sem.at[6], row_sem.at[7], (t, r_prev))
    sd_dn.start()
    arrived_delta(2, 1)
    back(2, 4, 4, 1)
    back(1, 2, 2, 1)
    time_grads(2, g_2, 0)
    between[2].start()
    arrived_delta(1, 1)
    back(1, 4, 4, 1)
    back(0, 0, 4, 1)
    time_grads(1, g_1, 0)
    between[1].start()
    add_cores(2)
    arrived_delta(0, 1)
    back(0, 4, 4, 1)
    sd_up = remote(sd.at[:, 192:256], sd_lo, row_sem.at[4], row_sem.at[5], (t, r_next))
    sd_up.start()
    time_grads(0, g_0, 0)
    between[0].start()
    add_cores(1)

    def spatial_grads(i, ref):
        rows = xs[:, 64 * i : 64 * i + 256, :].reshape(2048, 768)
        total = dot(dT[0:256, :], rows)
        for j in range(3):
            put(ref, j, total[:, 256 * j : 256 * j + 256])

    for f in range(F):
        dT[0:256, 256 * f : 256 * f + 256] = sd[f].T
    spatial_grads(0, g_x)
    between[4].start()
    spatial_grads(1, g_y)
    between[5].start()
    add_cores(0)
    add_cores(4)
    spatial_grads(2, g_z)
    between[6].start()
    add_cores(5)

    @pl.loop(0, F)
    def _(f):
        v = sd[f]
        left, right = columns(v)
        ys[f, 64:320, 0:256] = right
        ys[f, 64:320, 256:512] = v
        ys[f, 64:320, 512:768] = left

    add_cores(6)
    sd_up.wait()
    sd_dn.wait()

    @pl.when(r == 0)
    def _():
        sd_lo[...] = jnp.zeros_like(sd_lo)

    @pl.when(r == 15)
    def _():
        sd_hi[...] = jnp.zeros_like(sd_hi)

    @pl.loop(0, F)
    def _(f):
        for ref, at in ((sd_lo, 0), (sd_hi, 320)):
            v = ref[f]
            left, right = columns(v)
            ys[f, at : at + 64, 0:256] = right
            ys[f, at : at + 64, 256:512] = v
            ys[f, at : at + 64, 512:768] = left
    def input_grads(f, n, q):
        cat = jnp.concatenate(
            [
                ys[f : f + n, 64 * (2 - i) + HALF * q : 64 * (2 - i) + HALF * q + HALF, :].reshape(
                    n * HALF, 768
                )
                for i in range(3)
            ],
            axis=1,
        )
        total = dot(cat, wsT[...].reshape(2304, 256)) + past(cot, f, n, q).astype(F32)
        gin[f : f + n, half(q)] = total.astype(BF).reshape(n, HALF, N)

    def outputs(f, n, q):
        total = temporal(3, f, n, q) + past(lat, f, n, q).astype(F32)
        out[f : f + n, half(q)] = total.astype(BF).reshape(n, HALF, N)

    input_grads(0, 4, 0)
    input_grads(4, 4, 0)
    input_grads(0, 4, 1)
    input_grads(4, 4, 1)
    gin_store = pltpu.make_async_copy(gin, gin_hbm, load_sem.at[4])
    gin_store.start()
    for k in (3, 2, 1, 0):
        add_z(k, mb_t, 2 * k)
        to_owner(2 * k, 2 * k + 2, mb_t, rc_t, 0, 8)
    arrived_state(3, 0)
    outputs(0, 4, 0)
    outputs(4, 4, 0)
    add_z(4, mb_s, 0)
    to_owner(0, 3, mb_s, rc_s, 1, 0)
    own_sum(8, mb_t, rc_t, mc_t, 0, 8)
    arrived_state(3, 1)
    outputs(0, 4, 1)
    outputs(4, 4, 1)
    out_store = pltpu.make_async_copy(out, out_hbm, load_sem.at[5])
    out_store.start()
    add_z(5, mb_s, 3)
    to_owner(3, 6, mb_s, rc_s, 1, 0)
    add_z(6, mb_s, 6)
    to_owner(6, 9, mb_s, rc_s, 1, 0)
    own_sum(9, mb_s, rc_s, mc_s, 1, 0)
    for n in range(7):
        sent_z(n)
    finish(8, mb_t, rc_t, mc_t, 0, 8, gt_out)
    finish(9, mb_s, rc_s, mc_s, 1, 0, gs_out)
    gin_store.wait()
    out_store.wait()
def handed_on(*refs):
    sem = refs[-1]
    parts = [(k, slice(2 * p, 2 * p + 2)) for k in (0, 1) for p in range(4)]
    parts += [(2, slice(0, 9)), (3, slice(0, 8))]
    loads = [
        pltpu.make_async_copy(refs[k].at[at], refs[8 + k].at[at], sem.at[0, n])
        for n, (k, at) in enumerate(parts)
    ]
    stores = [
        pltpu.make_async_copy(refs[8 + k].at[at], refs[4 + k].at[at], sem.at[1, n])
        for n, (k, at) in enumerate(parts)
    ]
    for copy in loads:
        copy.start()
    for load, store in zip(loads, stores):
        load.wait()
        store.start()
    for copy in stores:
        copy.wait()


def shards(latents, cotangent, w_spatial, w_time):
    shape = latents.shape
    vmem = pl.BlockSpec(memory_space=pltpu.VMEM)
    hbm = pl.BlockSpec(memory_space=pl.ANY)
    V = pltpu.VMEM
    DMA = pltpu.SemaphoreType.DMA
    sizes = (2, 2, 2, 2, 3, 3, 3)
    scratch = [
        V((F, N, N), BF), V((F, N, N), BF), V((3, 768, N), BF), V((4, 512, N), BF),
        V((F, N, N), BF), V((F, N, N), BF),
        V((F, 384, 768), BF), V((F, 384, 768), BF),
        V((F, 64, N), BF), V((F, 64, N), BF), V((F, 64, N), BF), V((F, 64, N), BF),
        V((9, N, N), BF), V((10, N, N), BF), V((12, N, N), BF), V((16, N, N), BF),
        V((4, F, N, N), F32),
        V((9, N, N), BF), V((10, N, N), BF), V((12, N, N), BF), V((F, N, N), BF), V((F, N, N), BF),
        V((512, 2048), BF), V((3, 768, 256), BF), V((4, 512, 256), BF),
        *[V((2, 8, n, 16, N), BF) for n in sizes],
        *[V((8, n, 16, N), BF) for n in sizes],
        *[V((8, n, 16, N), BF) for n in sizes],
        *[V((8, n, 16, N), BF) for n in sizes],
        V((8, 16, N), BF), V((9, 16, N), BF),
        V((16, 16, N), BF), V((16, 16, N), BF),
        V((8, 16, N), BF), V((9, 16, N), BF),
        DMA((6,)), DMA((8,)), DMA((2, 8)), DMA((2, 8)), DMA((7, 2)),
        DMA((7, 8)), DMA((7, 8)), DMA((2, 9)), DMA((2, 16)), DMA((2, 16)), DMA((2, 9)),
    ]
    results = [
        jax.ShapeDtypeStruct((F, N, N), BF),
        jax.ShapeDtypeStruct((F, N, N), BF),
        jax.ShapeDtypeStruct((9, 16, N), F32),
        jax.ShapeDtypeStruct((8, 16, N), F32),
    ]
    held = pl.pallas_call(
        kernel,
        out_shape=results,
        in_specs=[hbm] * 4,
        out_specs=[hbm, hbm, vmem, vmem],
        scratch_shapes=scratch,
        compiler_params=pltpu.CompilerParams(
            collective_id=0, has_side_effects=True, vmem_limit_bytes=60 * 1024 * 1024
        ),
        cost_estimate=pl.CostEstimate(
            flops=51 * 2 * 2048 * N * N, bytes_accessed=7 * 1024 * 1024, transcendentals=4 * 2048 * N
        ),
    )(
        latents.reshape(F, N, N), cotangent.reshape(F, N, N),
        w_spatial.reshape(3, 768, N), w_time.reshape(4, 512, N),
    )
    out, gin, gs, gt = pl.pallas_call(
        handed_on,
        out_shape=results,
        in_specs=[hbm] * 4,
        out_specs=[hbm] * 4,
        scratch_shapes=[*[V(x.shape, x.dtype) for x in results], DMA((2, 10))],
        cost_estimate=pl.CostEstimate(flops=0, bytes_accessed=5 * 1024 * 1024, transcendentals=0),
    )(*held)
    spatial = jnp.swapaxes(gs, 1, 2)
    time = jnp.swapaxes(gt, 1, 2).reshape(4, 2, N, 16)
    return out.reshape(shape), gin.reshape(shape), spatial, time


def solution(mesh):
    in_specs = (P("tm", "rows", None, None), P("tm", "rows", None, None), P(), P())
    out_specs = (
        P("tm", "rows", None, None),
        P("tm", "rows", None, None),
        P(None, None, "rows"),
        P(None, None, None, "rows"),
    )
    return jax.shard_map(shards, mesh=mesh, in_specs=in_specs, out_specs=out_specs, check_vma=False)
```

```python
import math

import jax
import jax.numpy as jnp
from jax import lax
from jax.experimental import pallas as pl
from jax.experimental.pallas import tpu as pltpu
from jax.sharding import PartitionSpec as P

MESH = pl.DeviceIdType.MESH
F = 8
N = 256
HALF = 128
BF = jnp.bfloat16
F32 = jnp.float32


def dot(a, b):
    return lax.dot_general(a, b, (((1,), (0,)), ((), ())), preferred_element_type=F32)


def columns(v):
    wide = v.astype(F32)
    n = wide.shape[0]
    col = lax.rem(lax.broadcasted_iota(jnp.int32, wide.shape, 0), 64)
    left = jnp.where(col == 0, 0.0, pltpu.roll(wide, 1, 0)).astype(BF)
    right = jnp.where(col == 63, 0.0, pltpu.roll(wide, n - 1, 0)).astype(BF)
    return left, right


def kernel(
    lat_in, cot_in, ws_in, wt_in,
    out, gin, gs_out, gt_out,
    lat, cot, ws, wt,
    xs, ys, lat_lo, lat_hi, sd_lo, sd_hi,
    s0, s1, s2, s3, slope, d0, d1, d2, d3h, sd, dT, wsT, wtT,
    g_0, g_1, g_2, g_3, g_x, g_y, g_z,
    ra_0, ra_1, ra_2, ra_3, ra_x, ra_y, ra_z,
    ma_0, ma_1, ma_2, ma_3, ma_x, ma_y, ma_z,
    rb_0, rb_1, rb_2, rb_3, rb_x, rb_y, rb_z,
    mb_t, mb_s, rc_t, rc_s, mc_t, mc_s,
    load_sem, row_sem, tm_send, tm_recv, a_sem, b_send, b_recv, c_send, c_recv, h_send, h_recv,
):
    t = lax.axis_index("tm")
    r = lax.axis_index("rows")
    z = r // 2
    c = lax.rem(r, 2)
    tm_next = lax.rem(t + 1, 16)
    tm_prev = lax.rem(t + 15, 16)
    r_next = lax.rem(r + 1, 16)
    r_prev = lax.rem(r + 15, 16)
    sibling = r + 1 - 2 * c
    far = lax.rem(r + 15 + 2 * c, 16)
    states = (s0, s1, s2, s3)
    deltas = (d0, d1, d2, d3h)
    factor = 1.0 / math.sqrt(524288.0)
    barrier = pltpu.get_barrier_semaphore()
    for k in (1, 15, 2, 14, 3, 13, 4, 12, 5, 11, 6, 10, 7, 9, 8):
        pl.semaphore_signal(barrier, inc=1, device_id=(lax.rem(t + k, 16), r), device_id_type=MESH)
    for k in range(1, 8):
        pl.semaphore_signal(
            barrier, inc=1, device_id=(t, lax.rem(r + 2 * k, 16)), device_id_type=MESH
        )
    pl.semaphore_signal(barrier, inc=1, device_id=(t, sibling), device_id_type=MESH)
    pl.semaphore_signal(barrier, inc=1, device_id=(t, far), device_id_type=MESH)

    loads = [
        pltpu.make_async_copy(src, dst, load_sem.at[k])
        for k, (src, dst) in enumerate(((lat_in, lat), (ws_in, ws), (wt_in, wt), (cot_in, cot)))
    ]
    for copy in loads:
        copy.start()
    pl.semaphore_wait(barrier, 24)

    def remote(src, dst, send, recv, device):
        return pltpu.make_async_remote_copy(
            src_ref=src, dst_ref=dst, send_sem=send, recv_sem=recv, device_id=device,
            device_id_type=MESH,
        )
    lat_up = remote(lat_in.at[:, 192:256], lat_lo, row_sem.at[0], row_sem.at[1], (t, r_next))
    lat_dn = remote(lat_in.at[:, 0:64], lat_hi, row_sem.at[2], row_sem.at[3], (t, r_prev))
    lat_up.start()
    lat_dn.start()

    def half(q):
        return slice(HALF * q, HALF * q + HALF)

    state_up = [
        [
            remote(
                states[k].at[8 : 8 + 2**k, half(q)], states[k].at[0 : 2**k, half(q)],
                tm_send.at[q, k], tm_recv.at[q, k], (tm_next, r),
            )
            for k in range(4)
        ]
        for q in range(2)
    ]
    delta_dn = [
        [
            remote(
                deltas[k].at[0 : 2**k, half(q)], deltas[k].at[8 : 8 + 2**k, half(q)],
                tm_send.at[q, 4 + k], tm_recv.at[q, 4 + k], (tm_prev, r),
            )
            for k in range(3)
        ]
        + [
            remote(
                cot_in.at[:, half(q)], d3h.at[:, half(q)], tm_send.at[q, 7], tm_recv.at[q, 7],
                (tm_prev, r),
            )
        ]
        for q in range(2)
    ]
    delta_dn[0][3].start()
    delta_dn[1][3].start()

    loads[0].wait()

    @pl.loop(0, F)
    def _(f):
        v = lat[f]
        left, right = columns(v)
        xs[f, 64:320, 0:256] = left
        xs[f, 64:320, 256:512] = v
        xs[f, 64:320, 512:768] = right

    loads[1].wait()
    lat_up.wait()
    lat_dn.wait()

    @pl.when(r == 0)
    def _():
        lat_lo[...] = jnp.zeros_like(lat_lo)

    @pl.when(r == 15)
    def _():
        lat_hi[...] = jnp.zeros_like(lat_hi)

    @pl.loop(0, F)
    def _(f):
        for ref, at in ((lat_lo, 0), (lat_hi, 320)):
            v = ref[f]
            left, right = columns(v)
            xs[f, at : at + 64, 0:256] = left
            xs[f, at : at + 64, 256:512] = v
            xs[f, at : at + 64, 512:768] = right

    def activate(k, f, n, q, v):
        sigma = 0.5 + 0.5 * jnp.tanh(0.5 * v)
        state = v * sigma
        states[k][2**k + f : 2**k + f + n, half(q)] = state.astype(BF).reshape(n, HALF, N)
        slope[k, f : f + n, half(q)] = (sigma + state * (1.0 - sigma)).reshape(n, HALF, N)

    def conv(f, n, q):
        cat = jnp.concatenate(
            [
                xs[f : f + n, 64 * i + HALF * q : 64 * i + HALF * q + HALF, :].reshape(n * HALF, 768)
                for i in range(3)
            ],
            axis=1,
        )
        activate(0, f, n, q, dot(cat, ws[...].reshape(2304, 256)))

    def past(ref, at, n, q):
        return ref[at : at + n, half(q)].reshape(n * HALF, N)

    def temporal(k, f, n, q):
        cat = jnp.concatenate(
            [past(states[k], f + 2**k, n, q), past(states[k], f, n, q)], axis=1
        )
        return dot(cat, wt[k])

    def forward(k, f, n, q):
        activate(k + 1, f, n, q, temporal(k, f, n, q))

    def arrived_state(k, q):
        state_up[q][k].wait()

        @pl.when(t == 0)
        def _():
            states[k][0 : 2**k, half(q)] = jnp.zeros((2**k, HALF, N), BF)
    for q in range(2):
        conv(4, 4, q)
        state_up[q][0].start()
        conv(0, 4, q)
        if q == 0:
            loads[2].wait()
        forward(0, 4, 4, q)
        state_up[q][1].start()
        forward(0, 1, 3, q)
        forward(1, 4, 4, q)
        state_up[q][2].start()
        forward(1, 3, 1, q)
    for i in range(3):
        for j in range(3):
            wsT[i, 256 * j : 256 * j + 256, :] = ws[i, 256 * j : 256 * j + 256, :].T

    @pl.loop(0, 4)
    def _(k):
        wtT[k, 0:256, :] = wt[k, 0:256, :].T
        wtT[k, 256:512, :] = wt[k, 256:512, :].T

    loads[3].wait()

    def back(k, f, n, q):
        source = cot if k == 3 else deltas[k]
        later = past(d3h, f, n, q) if k == 3 else past(deltas[k], f + 2**k, n, q)
        total = dot(jnp.concatenate([past(source, f, n, q), later], axis=1), wtT[k])
        value = (total * past(slope.at[k], f, n, q)).astype(BF)
        target = sd if k == 0 else deltas[k - 1]
        target[f : f + n, half(q)] = value.reshape(n, HALF, N)

    def arrived_delta(k, q):
        delta_dn[q][k].wait()
        at = 0 if k == 3 else 8

        @pl.when(t == 15)
        def _():
            deltas[k][at : at + 2**k, half(q)] = jnp.zeros((2**k, HALF, N), BF)

    for q in range(2):
        arrived_state(0, q)
        forward(0, 0, 1, q)
        arrived_state(1, q)
        forward(1, 0, 3, q)
        forward(2, 4, 4, q)
        arrived_state(2, q)
        forward(2, 0, 4, q)
        state_up[q][3].start()
        arrived_delta(3, q)
        back(3, 0, 4, q)
        delta_dn[q][2].start()
        back(3, 4, 4, q)
        back(2, 0, 4, q)
        delta_dn[q][1].start()
        back(1, 0, 2, q)
        delta_dn[q][0].start()

    def put(ref, tap, value):
        for part in range(16):
            ref[part % 2, part // 2, tap] = value[16 * part : 16 * part + 16].astype(BF)

    def time_grads(k, ref, tap):
        d = 2**k
        for f in range(F):
            src = cot if k == 3 else deltas[k]
            dT[0:256, 256 * f : 256 * f + 256] = src[f].T
            other = d3h[f] if k == 3 else deltas[k][f + d]
            dT[256:512, 256 * f : 256 * f + 256] = other.T
        both = dot(dT[...], states[k][d : d + F].reshape(2048, N))
        put(ref, tap, both[0:256])
        put(ref, tap + 1, both[256:512])

    groups = [
        (g_0, ra_0, ma_0, rb_0),
        (g_1, ra_1, ma_1, rb_1),
        (g_2, ra_2, ma_2, rb_2),
        (g_3, ra_3, ma_3, rb_3),
        (g_x, ra_x, ma_x, rb_x),
        (g_y, ra_y, ma_y, rb_y),
        (g_z, ra_z, ma_z, rb_z),
    ]
    between = [
        remote(g.at[1 - c], ra, a_sem.at[n, 0], a_sem.at[n, 1], (t, sibling))
        for n, (g, ra, _, _) in enumerate(groups)
    ]

    def z_copies(n):
        _, _, ma, rb = groups[n]
        return [
            remote(
                ma.at[lax.rem(z + k, 8)], rb.at[z], b_send.at[n, k], b_recv.at[n, z],
                (t, lax.rem(r + 2 * k, 16)),
            )
            for k in (4, 3, 5, 2, 6, 1, 7)
        ]

    def add_cores(n):
        g, ra, ma, rb = groups[n]
        between[n].wait()

        @pl.loop(0, 8)
        def _(p):
            ma[p] = (g[c, p].astype(F32) + ra[p].astype(F32)).astype(BF)

        for copy in z_copies(n):
            copy.start()
        rb[z] = ma[z]

    def add_z(n, mb, at):
        taps = groups[n][0].shape[2]
        rb = groups[n][3]
        for k in range(1, 8):
            source = lax.rem(z + 8 - k, 8)
            remote(
                rb.at[source], rb.at[source], b_send.at[n, k], b_recv.at[n, source],
                (t, lax.rem(r + 16 - 2 * k, 16)),
            ).wait_recv()
        total = rb[0].astype(F32)
        for p in range(1, 8):
            total = total + rb[p].astype(F32)
        mb[at : at + taps] = total.astype(BF)

    def sent_z(n):
        for copy in z_copies(n):
            copy.wait_send()

    def to_owner(low, high, mb, rc, group, first):
        for k in range(low, high):
            owner = first + k

            @pl.when(t != owner)
            def _():
                remote(
                    mb.at[k], rc.at[t], c_send.at[group, k], c_recv.at[group, t], (owner, r)
                ).start()

    def own_sum(taps, mb, rc, mc, group, first):
        mine = t - first

        @pl.when((t >= first) & (t < first + taps))
        def _():
            rc[t] = mb[mine]
            for k in range(1, 16):
                source = lax.rem(t + k, 16)
                remote(
                    rc.at[source], rc.at[source], c_send.at[group, 0], c_recv.at[group, source],
                    (source, r),
                ).wait_recv()
            total = rc[0].astype(F32)
            for p in range(1, 16):
                total = total + rc[p].astype(F32)
            mc[mine] = total.astype(BF)
            for k in range(1, 16):
                remote(
                    mc.at[mine], mc.at[mine], h_send.at[group, k], h_recv.at[group, mine],
                    (lax.rem(t + k, 16), r),
                ).start()

    def finish(taps, mb, rc, mc, group, first, target):
        mine = t - first
        for k in range(taps):
            owner = first + k

            @pl.when(t != owner)
            def _():
                remote(
                    mb.at[k], rc.at[t], c_send.at[group, k], c_recv.at[group, t], (owner, r)
                ).wait_send()
                remote(
                    mc.at[k], mc.at[k], h_send.at[group, 0], h_recv.at[group, k], (owner, r)
                ).wait_recv()

        target[...] = mc[...].astype(F32) * factor

        @pl.when((t >= first) & (t < first + taps))
        def _():
            for k in range(1, 16):
                remote(
                    mc.at[mine], mc.at[mine], h_send.at[group, k], h_recv.at[group, mine],
                    (lax.rem(t + k, 16), r),
                ).wait_send()
    time_grads(3, g_3, 0)
    between[3].start()
    arrived_delta(2, 0)
    back(2, 4, 4, 0)
    back(1, 2, 2, 0)
    arrived_delta(1, 0)
    back(1, 4, 4, 0)
    back(0, 0, 4, 0)
    add_cores(3)
    arrived_delta(0, 0)
    back(0, 4, 4, 0)
    sd_dn = remote(sd.at[:, 0:64], sd_hi, row_sem.at[6], row_sem.at[7], (t, r_prev))
    sd_dn.start()
    arrived_delta(2, 1)
    back(2, 4, 4, 1)
    back(1, 2, 2, 1)
    time_grads(2, g_2, 0)
    between[2].start()
    arrived_delta(1, 1)
    back(1, 4, 4, 1)
    back(0, 0, 4, 1)
    time_grads(1, g_1, 0)
    between[1].start()
    add_cores(2)
    arrived_delta(0, 1)
    back(0, 4, 4, 1)
    sd_up = remote(sd.at[:, 192:256], sd_lo, row_sem.at[4], row_sem.at[5], (t, r_next))
    sd_up.start()
    time_grads(0, g_0, 0)
    between[0].start()
    add_cores(1)

    def spatial_grads(i, ref):
        rows = xs[:, 64 * i : 64 * i + 256, :].reshape(2048, 768)
        total = dot(dT[0:256, :], rows)
        for j in range(3):
            put(ref, j, total[:, 256 * j : 256 * j + 256])

    for f in range(F):
        dT[0:256, 256 * f : 256 * f + 256] = sd[f].T
    spatial_grads(0, g_x)
    between[4].start()
    spatial_grads(1, g_y)
    between[5].start()
    add_cores(0)
    add_cores(4)
    spatial_grads(2, g_z)
    between[6].start()
    add_cores(5)

    @pl.loop(0, F)
    def _(f):
        v = sd[f]
        left, right = columns(v)
        ys[f, 64:320, 0:256] = right
        ys[f, 64:320, 256:512] = v
        ys[f, 64:320, 512:768] = left

    add_cores(6)
    sd_up.wait()
    sd_dn.wait()

    @pl.when(r == 0)
    def _():
        sd_lo[...] = jnp.zeros_like(sd_lo)

    @pl.when(r == 15)
    def _():
        sd_hi[...] = jnp.zeros_like(sd_hi)

    @pl.loop(0, F)
    def _(f):
        for ref, at in ((sd_lo, 0), (sd_hi, 320)):
            v = ref[f]
            left, right = columns(v)
            ys[f, at : at + 64, 0:256] = right
            ys[f, at : at + 64, 256:512] = v
            ys[f, at : at + 64, 512:768] = left
    def input_grads(f, n, q):
        cat = jnp.concatenate(
            [
                ys[f : f + n, 64 * (2 - i) + HALF * q : 64 * (2 - i) + HALF * q + HALF, :].reshape(
                    n * HALF, 768
                )
                for i in range(3)
            ],
            axis=1,
        )
        total = dot(cat, wsT[...].reshape(2304, 256)) + past(cot, f, n, q).astype(F32)
        gin[f : f + n, half(q)] = total.astype(BF).reshape(n, HALF, N)

    def outputs(f, n, q):
        total = temporal(3, f, n, q) + past(lat, f, n, q).astype(F32)
        out[f : f + n, half(q)] = total.astype(BF).reshape(n, HALF, N)

    input_grads(0, 4, 0)
    input_grads(4, 4, 0)
    input_grads(0, 4, 1)
    input_grads(4, 4, 1)
    for k in (3, 2, 1, 0):
        add_z(k, mb_t, 2 * k)
        to_owner(2 * k, 2 * k + 2, mb_t, rc_t, 0, 8)
    arrived_state(3, 0)
    outputs(0, 4, 0)
    outputs(4, 4, 0)
    add_z(4, mb_s, 0)
    to_owner(0, 3, mb_s, rc_s, 1, 0)
    own_sum(8, mb_t, rc_t, mc_t, 0, 8)
    arrived_state(3, 1)
    outputs(0, 4, 1)
    outputs(4, 4, 1)
    add_z(5, mb_s, 3)
    to_owner(3, 6, mb_s, rc_s, 1, 0)
    add_z(6, mb_s, 6)
    to_owner(6, 9, mb_s, rc_s, 1, 0)
    own_sum(9, mb_s, rc_s, mc_s, 1, 0)
    for n in range(7):
        sent_z(n)
    finish(8, mb_t, rc_t, mc_t, 0, 8, gt_out)
    finish(9, mb_s, rc_s, mc_s, 1, 0, gs_out)
def handed_on(*refs):
    sem = refs[-1]
    parts = [(k, slice(4 * p, 4 * p + 4)) for k in (0, 1) for p in range(2)]
    parts += [(2, slice(0, 9)), (3, slice(0, 8))]
    stores = [
        pltpu.make_async_copy(refs[k].at[at], refs[4 + k].at[at], sem.at[n])
        for n, (k, at) in enumerate(parts)
    ]
    for copy in stores:
        copy.start()
    for copy in stores:
        copy.wait()


def shards(latents, cotangent, w_spatial, w_time):
    shape = latents.shape
    vmem = pl.BlockSpec(memory_space=pltpu.VMEM)
    hbm = pl.BlockSpec(memory_space=pl.ANY)
    V = pltpu.VMEM
    DMA = pltpu.SemaphoreType.DMA
    sizes = (2, 2, 2, 2, 3, 3, 3)
    scratch = [
        V((F, N, N), BF), V((F, N, N), BF), V((3, 768, N), BF), V((4, 512, N), BF),
        V((F, 384, 768), BF), V((F, 384, 768), BF),
        V((F, 64, N), BF), V((F, 64, N), BF), V((F, 64, N), BF), V((F, 64, N), BF),
        V((9, N, N), BF), V((10, N, N), BF), V((12, N, N), BF), V((16, N, N), BF),
        V((4, F, N, N), F32),
        V((9, N, N), BF), V((10, N, N), BF), V((12, N, N), BF), V((F, N, N), BF), V((F, N, N), BF),
        V((512, 2048), BF), V((3, 768, 256), BF), V((4, 512, 256), BF),
        *[V((2, 8, n, 16, N), BF) for n in sizes],
        *[V((8, n, 16, N), BF) for n in sizes],
        *[V((8, n, 16, N), BF) for n in sizes],
        *[V((8, n, 16, N), BF) for n in sizes],
        V((8, 16, N), BF), V((9, 16, N), BF),
        V((16, 16, N), BF), V((16, 16, N), BF),
        V((8, 16, N), BF), V((9, 16, N), BF),
        DMA((4,)), DMA((8,)), DMA((2, 8)), DMA((2, 8)), DMA((7, 2)),
        DMA((7, 8)), DMA((7, 8)), DMA((2, 9)), DMA((2, 16)), DMA((2, 16)), DMA((2, 9)),
    ]
    results = [
        jax.ShapeDtypeStruct((F, N, N), BF),
        jax.ShapeDtypeStruct((F, N, N), BF),
        jax.ShapeDtypeStruct((9, 16, N), F32),
        jax.ShapeDtypeStruct((8, 16, N), F32),
    ]
    held = pl.pallas_call(
        kernel,
        out_shape=[V(x.shape, x.dtype) for x in results],
        in_specs=[hbm] * 4,
        out_specs=[vmem] * 4,
        scratch_shapes=scratch,
        compiler_params=pltpu.CompilerParams(
            collective_id=0, has_side_effects=True, vmem_limit_bytes=57 * 1024 * 1024
        ),
        cost_estimate=pl.CostEstimate(
            flops=51 * 2 * 2048 * N * N, bytes_accessed=7 * 1024 * 1024, transcendentals=4 * 2048 * N
        ),
    )(
        latents.reshape(F, N, N), cotangent.reshape(F, N, N),
        w_spatial.reshape(3, 768, N), w_time.reshape(4, 512, N),
    )
    out, gin, gs, gt = pl.pallas_call(
        handed_on,
        out_shape=results,
        in_specs=[vmem] * 4,
        out_specs=[hbm] * 4,
        scratch_shapes=[DMA((6,))],
        cost_estimate=pl.CostEstimate(flops=0, bytes_accessed=5 * 1024 * 1024, transcendentals=0),
    )(*[pltpu.with_memory_space_constraint(x, V) for x in held])
    spatial = jnp.swapaxes(gs, 1, 2)
    time = jnp.swapaxes(gt, 1, 2).reshape(4, 2, N, 16)
    return out.reshape(shape), gin.reshape(shape), spatial, time


def solution(mesh):
    in_specs = (P("tm", "rows", None, None), P("tm", "rows", None, None), P(), P())
    out_specs = (
        P("tm", "rows", None, None),
        P("tm", "rows", None, None),
        P(None, None, "rows"),
        P(None, None, None, "rows"),
    )
    return jax.shard_map(shards, mesh=mesh, in_specs=in_specs, out_specs=out_specs, check_vma=False)
```

```python
import math

import jax
import jax.numpy as jnp
from jax import lax
from jax.experimental import pallas as pl
from jax.experimental.pallas import tpu as pltpu
from jax.sharding import PartitionSpec as P

MESH = pl.DeviceIdType.MESH
F = 8
N = 256
HALF = 128
BF = jnp.bfloat16
F32 = jnp.float32


def dot(a, b):
    return lax.dot_general(a, b, (((1,), (0,)), ((), ())), preferred_element_type=F32)


def columns(v):
    wide = v.astype(F32)
    n = wide.shape[0]
    col = lax.rem(lax.broadcasted_iota(jnp.int32, wide.shape, 0), 64)
    left = jnp.where(col == 0, 0.0, pltpu.roll(wide, 1, 0)).astype(BF)
    right = jnp.where(col == 63, 0.0, pltpu.roll(wide, n - 1, 0)).astype(BF)
    return left, right


def kernel(
    lat_in, cot_in, ws_in, wt_in,
    out, gin, gs_out, gt_out,
    lat, cot, ws, wt,
    xs, ys, lat_lo, lat_hi, sd_lo, sd_hi,
    s0, s1, s2, s3, slope, d0, d1, d2, d3h, sd, dT, wsT, wtT,
    g_0, g_1, g_2, g_3, g_x, g_y, g_z,
    ra_0, ra_1, ra_2, ra_3, ra_x, ra_y, ra_z,
    ma_0, ma_1, ma_2, ma_3, ma_x, ma_y, ma_z,
    rb_0, rb_1, rb_2, rb_3, rb_x, rb_y, rb_z,
    mb_t, mb_s, rc_t, rc_s, mc_t, mc_s,
    load_sem, row_sem, tm_send, tm_recv, a_sem, b_send, b_recv, c_send, c_recv, h_send, h_recv,
):
    t = lax.axis_index("tm")
    r = lax.axis_index("rows")
    z = r // 2
    c = lax.rem(r, 2)
    tm_next = lax.rem(t + 1, 16)
    tm_prev = lax.rem(t + 15, 16)
    r_next = lax.rem(r + 1, 16)
    r_prev = lax.rem(r + 15, 16)
    sibling = r + 1 - 2 * c
    far = lax.rem(r + 15 + 2 * c, 16)
    states = (s0, s1, s2, s3)
    deltas = (d0, d1, d2, d3h)
    factor = 1.0 / math.sqrt(524288.0)
    barrier = pltpu.get_barrier_semaphore()
    for k in (1, 15, 2, 14, 3, 13, 4, 12, 5, 11, 6, 10, 7, 9, 8):
        pl.semaphore_signal(barrier, inc=1, device_id=(lax.rem(t + k, 16), r), device_id_type=MESH)
    for k in range(1, 8):
        pl.semaphore_signal(
            barrier, inc=1, device_id=(t, lax.rem(r + 2 * k, 16)), device_id_type=MESH
        )
    pl.semaphore_signal(barrier, inc=1, device_id=(t, sibling), device_id_type=MESH)
    pl.semaphore_signal(barrier, inc=1, device_id=(t, far), device_id_type=MESH)

    loads = [
        pltpu.make_async_copy(src, dst, load_sem.at[k])
        for k, (src, dst) in enumerate(((lat_in, lat), (ws_in, ws), (wt_in, wt), (cot_in, cot)))
    ]
    for copy in loads:
        copy.start()
    pl.semaphore_wait(barrier, 24)

    def remote(src, dst, send, recv, device):
        return pltpu.make_async_remote_copy(
            src_ref=src, dst_ref=dst, send_sem=send, recv_sem=recv, device_id=device,
            device_id_type=MESH,
        )
    lat_up = remote(lat_in.at[:, 192:256], lat_lo, row_sem.at[0], row_sem.at[1], (t, r_next))
    lat_dn = remote(lat_in.at[:, 0:64], lat_hi, row_sem.at[2], row_sem.at[3], (t, r_prev))
    lat_up.start()
    lat_dn.start()

    def half(q):
        return slice(HALF * q, HALF * q + HALF)

    state_up = [
        [
            remote(
                states[k].at[8 : 8 + 2**k, half(q)], states[k].at[0 : 2**k, half(q)],
                tm_send.at[q, k], tm_recv.at[q, k], (tm_next, r),
            )
            for k in range(4)
        ]
        for q in range(2)
    ]
    delta_dn = [
        [
            remote(
                deltas[k].at[0 : 2**k, half(q)], deltas[k].at[8 : 8 + 2**k, half(q)],
                tm_send.at[q, 4 + k], tm_recv.at[q, 4 + k], (tm_prev, r),
            )
            for k in range(3)
        ]
        + [
            remote(
                cot_in.at[:, half(q)], d3h.at[:, half(q)], tm_send.at[q, 7], tm_recv.at[q, 7],
                (tm_prev, r),
            )
        ]
        for q in range(2)
    ]
    delta_dn[0][3].start()
    delta_dn[1][3].start()

    loads[0].wait()

    @pl.loop(0, F)
    def _(f):
        v = lat[f]
        left, right = columns(v)
        xs[f, 64:320, 0:256] = left
        xs[f, 64:320, 256:512] = v
        xs[f, 64:320, 512:768] = right

    loads[1].wait()
    lat_up.wait()
    lat_dn.wait()

    @pl.when(r == 0)
    def _():
        lat_lo[...] = jnp.zeros_like(lat_lo)

    @pl.when(r == 15)
    def _():
        lat_hi[...] = jnp.zeros_like(lat_hi)

    @pl.loop(0, F)
    def _(f):
        for ref, at in ((lat_lo, 0), (lat_hi, 320)):
            v = ref[f]
            left, right = columns(v)
            xs[f, at : at + 64, 0:256] = left
            xs[f, at : at + 64, 256:512] = v
            xs[f, at : at + 64, 512:768] = right

    def activate(k, f, n, q, v):
        sigma = 0.5 + 0.5 * jnp.tanh(0.5 * v)
        state = v * sigma
        states[k][2**k + f : 2**k + f + n, half(q)] = state.astype(BF).reshape(n, HALF, N)
        slope[k, f : f + n, half(q)] = (sigma + state * (1.0 - sigma)).reshape(n, HALF, N)

    def conv(f, n, q):
        cat = jnp.concatenate(
            [
                xs[f : f + n, 64 * i + HALF * q : 64 * i + HALF * q + HALF, :].reshape(n * HALF, 768)
                for i in range(3)
            ],
            axis=1,
        )
        activate(0, f, n, q, dot(cat, ws[...].reshape(2304, 256)))

    def past(ref, at, n, q):
        return ref[at : at + n, half(q)].reshape(n * HALF, N)

    def temporal(k, f, n, q):
        cat = jnp.concatenate(
            [past(states[k], f + 2**k, n, q), past(states[k], f, n, q)], axis=1
        )
        return dot(cat, wt[k])

    def forward(k, f, n, q):
        activate(k + 1, f, n, q, temporal(k, f, n, q))

    def arrived_state(k, q):
        state_up[q][k].wait()

        @pl.when(t == 0)
        def _():
            states[k][0 : 2**k, half(q)] = jnp.zeros((2**k, HALF, N), BF)
    for q in range(2):
        conv(4, 4, q)
        state_up[q][0].start()
        conv(0, 4, q)
        if q == 0:
            loads[2].wait()
        forward(0, 4, 4, q)
        state_up[q][1].start()
        forward(0, 1, 3, q)
        forward(1, 4, 4, q)
        state_up[q][2].start()
        forward(1, 3, 1, q)
    for i in range(3):
        for j in range(3):
            wsT[i, 256 * j : 256 * j + 256, :] = ws[i, 256 * j : 256 * j + 256, :].T

    @pl.loop(0, 4)
    def _(k):
        wtT[k, 0:256, :] = wt[k, 0:256, :].T
        wtT[k, 256:512, :] = wt[k, 256:512, :].T

    loads[3].wait()

    def back(k, f, n, q):
        source = cot if k == 3 else deltas[k]
        later = past(d3h, f, n, q) if k == 3 else past(deltas[k], f + 2**k, n, q)
        total = dot(jnp.concatenate([past(source, f, n, q), later], axis=1), wtT[k])
        value = (total * past(slope.at[k], f, n, q)).astype(BF)
        target = sd if k == 0 else deltas[k - 1]
        target[f : f + n, half(q)] = value.reshape(n, HALF, N)

    def arrived_delta(k, q):
        delta_dn[q][k].wait()
        at = 0 if k == 3 else 8

        @pl.when(t == 15)
        def _():
            deltas[k][at : at + 2**k, half(q)] = jnp.zeros((2**k, HALF, N), BF)

    for q in range(2):
        arrived_state(0, q)
        forward(0, 0, 1, q)
        arrived_state(1, q)
        forward(1, 0, 3, q)
        forward(2, 4, 4, q)
        arrived_state(2, q)
        forward(2, 0, 4, q)
        state_up[q][3].start()
        arrived_delta(3, q)
        back(3, 0, 4, q)
        delta_dn[q][2].start()
        back(3, 4, 4, q)
        back(2, 0, 4, q)
        delta_dn[q][1].start()
        back(1, 0, 2, q)
        delta_dn[q][0].start()

    def put(ref, tap, value):
        for part in range(16):
            ref[part % 2, part // 2, tap] = value[16 * part : 16 * part + 16].astype(BF)

    def time_grads(k, ref, tap):
        d = 2**k
        for f in range(F):
            src = cot if k == 3 else deltas[k]
            dT[0:256, 256 * f : 256 * f + 256] = src[f].T
            other = d3h[f] if k == 3 else deltas[k][f + d]
            dT[256:512, 256 * f : 256 * f + 256] = other.T
        both = dot(dT[...], states[k][d : d + F].reshape(2048, N))
        put(ref, tap, both[0:256])
        put(ref, tap + 1, both[256:512])

    groups = [
        (g_0, ra_0, ma_0, rb_0),
        (g_1, ra_1, ma_1, rb_1),
        (g_2, ra_2, ma_2, rb_2),
        (g_3, ra_3, ma_3, rb_3),
        (g_x, ra_x, ma_x, rb_x),
        (g_y, ra_y, ma_y, rb_y),
        (g_z, ra_z, ma_z, rb_z),
    ]
    between = [
        remote(g.at[1 - c], ra, a_sem.at[n, 0], a_sem.at[n, 1], (t, sibling))
        for n, (g, ra, _, _) in enumerate(groups)
    ]

    def z_copies(n):
        _, _, ma, rb = groups[n]
        return [
            remote(
                ma.at[lax.rem(z + k, 8)], rb.at[z], b_send.at[n, k], b_recv.at[n, z],
                (t, lax.rem(r + 2 * k, 16)),
            )
            for k in (4, 3, 5, 2, 6, 1, 7)
        ]

    rings = (0, 1, 2)

    def upward(n, step):
        _, ra, ma, rb = groups[n]
        source = ma.at[lax.rem(z + 4, 8)] if step == 0 else ra.at[step - 1]
        return remote(
            source, rb.at[step], b_send.at[n, step], b_recv.at[n, step],
            (t, lax.rem(r + 2, 16)),
        )

    def downward(n, step):
        _, ra, ma, rb = groups[n]
        source = ma.at[lax.rem(z + 5, 8)] if step == 0 else ra.at[3 + step]
        return remote(
            source, rb.at[4 + step], b_send.at[n, 4 + step], b_recv.at[n, 4 + step],
            (t, lax.rem(r + 14, 16)),
        )

    def pass_on(n, step):
        _, ra, ma, rb = groups[n]
        upward(n, step - 1).wait_recv()
        ra[step - 1] = (
            ma[lax.rem(z + 4 - step, 8)].astype(F32) + rb[step - 1].astype(F32)
        ).astype(BF)
        upward(n, step).start()
        if step < 3:
            downward(n, step - 1).wait_recv()
            ra[3 + step] = (
                ma[lax.rem(z + 5 + step, 8)].astype(F32) + rb[3 + step].astype(F32)
            ).astype(BF)
            downward(n, step).start()

    def add_cores(n):
        g, ra, ma, rb = groups[n]
        between[n].wait()

        @pl.loop(0, 8)
        def _(p):
            ma[p] = (g[c, p].astype(F32) + ra[p].astype(F32)).astype(BF)

        if n in rings:
            upward(n, 0).start()
            downward(n, 0).start()
            return
        for copy in z_copies(n):
            copy.start()
        rb[z] = ma[z]

    def add_z(n, mb, at):
        taps = groups[n][0].shape[2]
        ma, rb = groups[n][2:]
        if n in rings:
            upward(n, 3).wait_recv()
            downward(n, 2).wait_recv()
            total = ma[z].astype(F32) + rb[3].astype(F32) + rb[6].astype(F32)
            mb[at : at + taps] = total.astype(BF)
            return
        for k in range(1, 8):
            source = lax.rem(z + 8 - k, 8)
            remote(
                rb.at[source], rb.at[source], b_send.at[n, k], b_recv.at[n, source],
                (t, lax.rem(r + 16 - 2 * k, 16)),
            ).wait_recv()
        total = rb[0].astype(F32)
        for p in range(1, 8):
            total = total + rb[p].astype(F32)
        mb[at : at + taps] = total.astype(BF)

    def sent_z(n):
        if n in rings:
            for step in range(4):
                upward(n, step).wait_send()
            for step in range(3):
                downward(n, step).wait_send()
            return
        for copy in z_copies(n):
            copy.wait_send()

    def to_owner(low, high, mb, rc, group, first):
        for k in range(low, high):
            owner = first + k

            @pl.when(t != owner)
            def _():
                remote(
                    mb.at[k], rc.at[t], c_send.at[group, k], c_recv.at[group, t], (owner, r)
                ).start()

    def own_sum(taps, mb, rc, mc, group, first):
        mine = t - first

        @pl.when((t >= first) & (t < first + taps))
        def _():
            rc[t] = mb[mine]
            for k in range(1, 16):
                source = lax.rem(t + k, 16)
                remote(
                    rc.at[source], rc.at[source], c_send.at[group, 0], c_recv.at[group, source],
                    (source, r),
                ).wait_recv()
            total = rc[0].astype(F32)
            for p in range(1, 16):
                total = total + rc[p].astype(F32)
            mc[mine] = total.astype(BF)
            for k in range(1, 16):
                remote(
                    mc.at[mine], mc.at[mine], h_send.at[group, k], h_recv.at[group, mine],
                    (lax.rem(t + k, 16), r),
                ).start()

    def finish(taps, mb, rc, mc, group, first, target):
        mine = t - first
        for k in range(taps):
            owner = first + k

            @pl.when(t != owner)
            def _():
                remote(
                    mb.at[k], rc.at[t], c_send.at[group, k], c_recv.at[group, t], (owner, r)
                ).wait_send()
                remote(
                    mc.at[k], mc.at[k], h_send.at[group, 0], h_recv.at[group, k], (owner, r)
                ).wait_recv()

        target[...] = mc[...].astype(F32) * factor

        @pl.when((t >= first) & (t < first + taps))
        def _():
            for k in range(1, 16):
                remote(
                    mc.at[mine], mc.at[mine], h_send.at[group, k], h_recv.at[group, mine],
                    (lax.rem(t + k, 16), r),
                ).wait_send()
    time_grads(3, g_3, 0)
    between[3].start()
    arrived_delta(2, 0)
    back(2, 4, 4, 0)
    back(1, 2, 2, 0)
    arrived_delta(1, 0)
    back(1, 4, 4, 0)
    back(0, 0, 4, 0)
    add_cores(3)
    arrived_delta(0, 0)
    back(0, 4, 4, 0)
    sd_dn = remote(sd.at[:, 0:64], sd_hi, row_sem.at[6], row_sem.at[7], (t, r_prev))
    sd_dn.start()
    arrived_delta(2, 1)
    back(2, 4, 4, 1)
    back(1, 2, 2, 1)
    time_grads(2, g_2, 0)
    between[2].start()
    arrived_delta(1, 1)
    back(1, 4, 4, 1)
    back(0, 0, 4, 1)
    time_grads(1, g_1, 0)
    between[1].start()
    add_cores(2)
    arrived_delta(0, 1)
    back(0, 4, 4, 1)
    sd_up = remote(sd.at[:, 192:256], sd_lo, row_sem.at[4], row_sem.at[5], (t, r_next))
    sd_up.start()
    add_cores(1)
    time_grads(0, g_0, 0)
    between[0].start()

    def spatial_grads(i, ref):
        rows = xs[:, 64 * i : 64 * i + 256, :].reshape(2048, 768)
        total = dot(dT[0:256, :], rows)
        for j in range(3):
            put(ref, j, total[:, 256 * j : 256 * j + 256])

    for f in range(F):
        dT[0:256, 256 * f : 256 * f + 256] = sd[f].T
    spatial_grads(0, g_x)
    between[4].start()
    spatial_grads(1, g_y)
    between[5].start()
    add_cores(0)
    add_cores(4)
    pass_on(2, 1)
    spatial_grads(2, g_z)
    between[6].start()
    pass_on(1, 1)
    add_cores(5)

    @pl.loop(0, F)
    def _(f):
        v = sd[f]
        left, right = columns(v)
        ys[f, 64:320, 0:256] = right
        ys[f, 64:320, 256:512] = v
        ys[f, 64:320, 512:768] = left

    add_cores(6)
    pass_on(2, 2)
    pass_on(0, 1)
    pass_on(1, 2)
    sd_up.wait()
    sd_dn.wait()

    @pl.when(r == 0)
    def _():
        sd_lo[...] = jnp.zeros_like(sd_lo)

    @pl.when(r == 15)
    def _():
        sd_hi[...] = jnp.zeros_like(sd_hi)

    @pl.loop(0, F)
    def _(f):
        for ref, at in ((sd_lo, 0), (sd_hi, 320)):
            v = ref[f]
            left, right = columns(v)
            ys[f, at : at + 64, 0:256] = right
            ys[f, at : at + 64, 256:512] = v
            ys[f, at : at + 64, 512:768] = left
    def input_grads(f, n, q):
        cat = jnp.concatenate(
            [
                ys[f : f + n, 64 * (2 - i) + HALF * q : 64 * (2 - i) + HALF * q + HALF, :].reshape(
                    n * HALF, 768
                )
                for i in range(3)
            ],
            axis=1,
        )
        total = dot(cat, wsT[...].reshape(2304, 256)) + past(cot, f, n, q).astype(F32)
        gin[f : f + n, half(q)] = total.astype(BF).reshape(n, HALF, N)

    def outputs(f, n, q):
        total = temporal(3, f, n, q) + past(lat, f, n, q).astype(F32)
        out[f : f + n, half(q)] = total.astype(BF).reshape(n, HALF, N)

    input_grads(0, 4, 0)
    pass_on(2, 3)
    pass_on(0, 2)
    pass_on(1, 3)
    input_grads(4, 4, 0)
    pass_on(0, 3)
    input_grads(0, 4, 1)
    input_grads(4, 4, 1)
    for k in (3, 2, 1, 0):
        add_z(k, mb_t, 2 * k)
        to_owner(2 * k, 2 * k + 2, mb_t, rc_t, 0, 8)
    arrived_state(3, 0)
    outputs(0, 4, 0)
    outputs(4, 4, 0)
    add_z(4, mb_s, 0)
    to_owner(0, 3, mb_s, rc_s, 1, 0)
    own_sum(8, mb_t, rc_t, mc_t, 0, 8)
    arrived_state(3, 1)
    outputs(0, 4, 1)
    outputs(4, 4, 1)
    add_z(5, mb_s, 3)
    to_owner(3, 6, mb_s, rc_s, 1, 0)
    add_z(6, mb_s, 6)
    to_owner(6, 9, mb_s, rc_s, 1, 0)
    own_sum(9, mb_s, rc_s, mc_s, 1, 0)
    for n in range(7):
        sent_z(n)
    finish(8, mb_t, rc_t, mc_t, 0, 8, gt_out)
    finish(9, mb_s, rc_s, mc_s, 1, 0, gs_out)
def handed_on(*refs):
    sem = refs[-1]
    parts = [(k, slice(4 * p, 4 * p + 4)) for k in (0, 1) for p in range(2)]
    parts += [(2, slice(0, 9)), (3, slice(0, 8))]
    stores = [
        pltpu.make_async_copy(refs[k].at[at], refs[4 + k].at[at], sem.at[n])
        for n, (k, at) in enumerate(parts)
    ]
    for copy in stores:
        copy.start()
    for copy in stores:
        copy.wait()


def shards(latents, cotangent, w_spatial, w_time):
    shape = latents.shape
    vmem = pl.BlockSpec(memory_space=pltpu.VMEM)
    hbm = pl.BlockSpec(memory_space=pl.ANY)
    V = pltpu.VMEM
    DMA = pltpu.SemaphoreType.DMA
    sizes = (2, 2, 2, 2, 3, 3, 3)
    scratch = [
        V((F, N, N), BF), V((F, N, N), BF), V((3, 768, N), BF), V((4, 512, N), BF),
        V((F, 384, 768), BF), V((F, 384, 768), BF),
        V((F, 64, N), BF), V((F, 64, N), BF), V((F, 64, N), BF), V((F, 64, N), BF),
        V((9, N, N), BF), V((10, N, N), BF), V((12, N, N), BF), V((16, N, N), BF),
        V((4, F, N, N), F32),
        V((9, N, N), BF), V((10, N, N), BF), V((12, N, N), BF), V((F, N, N), BF), V((F, N, N), BF),
        V((512, 2048), BF), V((3, 768, 256), BF), V((4, 512, 256), BF),
        *[V((2, 8, n, 16, N), BF) for n in sizes],
        *[V((8, n, 16, N), BF) for n in sizes],
        *[V((8, n, 16, N), BF) for n in sizes],
        *[V((8, n, 16, N), BF) for n in sizes],
        V((8, 16, N), BF), V((9, 16, N), BF),
        V((16, 16, N), BF), V((16, 16, N), BF),
        V((8, 16, N), BF), V((9, 16, N), BF),
        DMA((4,)), DMA((8,)), DMA((2, 8)), DMA((2, 8)), DMA((7, 2)),
        DMA((7, 8)), DMA((7, 8)), DMA((2, 9)), DMA((2, 16)), DMA((2, 16)), DMA((2, 9)),
    ]
    results = [
        jax.ShapeDtypeStruct((F, N, N), BF),
        jax.ShapeDtypeStruct((F, N, N), BF),
        jax.ShapeDtypeStruct((9, 16, N), F32),
        jax.ShapeDtypeStruct((8, 16, N), F32),
    ]
    held = pl.pallas_call(
        kernel,
        out_shape=[V(x.shape, x.dtype) for x in results],
        in_specs=[hbm] * 4,
        out_specs=[vmem] * 4,
        scratch_shapes=scratch,
        compiler_params=pltpu.CompilerParams(
            collective_id=0, has_side_effects=True, vmem_limit_bytes=57 * 1024 * 1024
        ),
        cost_estimate=pl.CostEstimate(
            flops=51 * 2 * 2048 * N * N, bytes_accessed=7 * 1024 * 1024, transcendentals=4 * 2048 * N
        ),
    )(
        latents.reshape(F, N, N), cotangent.reshape(F, N, N),
        w_spatial.reshape(3, 768, N), w_time.reshape(4, 512, N),
    )
    out, gin, gs, gt = pl.pallas_call(
        handed_on,
        out_shape=results,
        in_specs=[vmem] * 4,
        out_specs=[hbm] * 4,
        scratch_shapes=[DMA((6,))],
        cost_estimate=pl.CostEstimate(flops=0, bytes_accessed=5 * 1024 * 1024, transcendentals=0),
    )(*[pltpu.with_memory_space_constraint(x, V) for x in held])
    spatial = jnp.swapaxes(gs, 1, 2)
    time = jnp.swapaxes(gt, 1, 2).reshape(4, 2, N, 16)
    return out.reshape(shape), gin.reshape(shape), spatial, time


def solution(mesh):
    in_specs = (P("tm", "rows", None, None), P("tm", "rows", None, None), P(), P())
    out_specs = (
        P("tm", "rows", None, None),
        P("tm", "rows", None, None),
        P(None, None, "rows"),
        P(None, None, None, "rows"),
    )
    return jax.shard_map(shards, mesh=mesh, in_specs=in_specs, out_specs=out_specs, check_vma=False)
```

```python
import math

import jax
import jax.numpy as jnp
from jax import lax
from jax.experimental import pallas as pl
from jax.experimental.pallas import tpu as pltpu
from jax.sharding import PartitionSpec as P

MESH = pl.DeviceIdType.MESH
F = 8
N = 256
HALF = 128
BF = jnp.bfloat16
F32 = jnp.float32


def dot(a, b):
    return lax.dot_general(a, b, (((1,), (0,)), ((), ())), preferred_element_type=F32)


def columns(v):
    wide = v.astype(F32)
    n = wide.shape[0]
    col = lax.rem(lax.broadcasted_iota(jnp.int32, wide.shape, 0), 64)
    left = jnp.where(col == 0, 0.0, pltpu.roll(wide, 1, 0)).astype(BF)
    right = jnp.where(col == 63, 0.0, pltpu.roll(wide, n - 1, 0)).astype(BF)
    return left, right


def kernel(
    lat_in, cot_in, ws_in, wt_in,
    out, gin, gs_out, gt_out,
    lat, cot, ws, wt,
    xs, ys, lat_lo, lat_hi, sd_lo, sd_hi,
    s0, s1, s2, s3, slope, d0, d1, d2, d3h, sd, dT, wsT, wtT,
    g_0, g_1, g_2, g_3, g_x, g_y, g_z,
    ra_0, ra_1, ra_2, ra_3, ra_x, ra_y, ra_z,
    ma_0, ma_1, ma_2, ma_3, ma_x, ma_y, ma_z,
    rb_0, rb_1, rb_2, rb_3, rb_x, rb_y, rb_z,
    mb_t, mb_s, rc_t, rc_s, mc_t, mc_s,
    load_sem, row_sem, tm_send, tm_recv, a_sem, b_send, b_recv, c_send, c_recv, h_send, h_recv,
):
    t = lax.axis_index("tm")
    r = lax.axis_index("rows")
    z = r // 2
    c = lax.rem(r, 2)
    tm_next = lax.rem(t + 1, 16)
    tm_prev = lax.rem(t + 15, 16)
    r_next = lax.rem(r + 1, 16)
    r_prev = lax.rem(r + 15, 16)
    sibling = r + 1 - 2 * c
    far = lax.rem(r + 15 + 2 * c, 16)
    states = (s0, s1, s2, s3)
    deltas = (d0, d1, d2, d3h)
    factor = 1.0 / math.sqrt(524288.0)
    barrier = pltpu.get_barrier_semaphore()
    for k in (1, 15, 2, 14, 3, 13, 4, 12, 5, 11, 6, 10, 7, 9, 8):
        pl.semaphore_signal(barrier, inc=1, device_id=(lax.rem(t + k, 16), r), device_id_type=MESH)
    for k in range(1, 8):
        pl.semaphore_signal(
            barrier, inc=1, device_id=(t, lax.rem(r + 2 * k, 16)), device_id_type=MESH
        )
    pl.semaphore_signal(barrier, inc=1, device_id=(t, sibling), device_id_type=MESH)
    pl.semaphore_signal(barrier, inc=1, device_id=(t, far), device_id_type=MESH)

    loads = [
        pltpu.make_async_copy(src, dst, load_sem.at[k])
        for k, (src, dst) in enumerate(((lat_in, lat), (ws_in, ws), (wt_in, wt), (cot_in, cot)))
    ]
    for copy in loads:
        copy.start()
    pl.semaphore_wait(barrier, 24)

    def remote(src, dst, send, recv, device):
        return pltpu.make_async_remote_copy(
            src_ref=src, dst_ref=dst, send_sem=send, recv_sem=recv, device_id=device,
            device_id_type=MESH,
        )
    lat_up = remote(lat_in.at[:, 192:256], lat_lo, row_sem.at[0], row_sem.at[1], (t, r_next))
    lat_dn = remote(lat_in.at[:, 0:64], lat_hi, row_sem.at[2], row_sem.at[3], (t, r_prev))
    lat_up.start()
    lat_dn.start()

    def half(q):
        return slice(HALF * q, HALF * q + HALF)

    state_up = [
        [
            remote(
                states[k].at[8 : 8 + 2**k, half(q)], states[k].at[0 : 2**k, half(q)],
                tm_send.at[q, k], tm_recv.at[q, k], (tm_next, r),
            )
            for k in range(4)
        ]
        for q in range(2)
    ]
    delta_dn = [
        [
            remote(
                deltas[k].at[0 : 2**k, half(q)], deltas[k].at[8 : 8 + 2**k, half(q)],
                tm_send.at[q, 4 + k], tm_recv.at[q, 4 + k], (tm_prev, r),
            )
            for k in range(3)
        ]
        + [
            remote(
                cot_in.at[:, half(q)], d3h.at[:, half(q)], tm_send.at[q, 7], tm_recv.at[q, 7],
                (tm_prev, r),
            )
        ]
        for q in range(2)
    ]
    delta_dn[0][3].start()
    delta_dn[1][3].start()

    loads[0].wait()

    @pl.loop(0, F)
    def _(f):
        v = lat[f]
        left, right = columns(v)
        xs[f, 64:320, 0:256] = left
        xs[f, 64:320, 256:512] = v
        xs[f, 64:320, 512:768] = right

    loads[1].wait()
    lat_up.wait()
    lat_dn.wait()

    @pl.when(r == 0)
    def _():
        lat_lo[...] = jnp.zeros_like(lat_lo)

    @pl.when(r == 15)
    def _():
        lat_hi[...] = jnp.zeros_like(lat_hi)

    @pl.loop(0, F)
    def _(f):
        for ref, at in ((lat_lo, 0), (lat_hi, 320)):
            v = ref[f]
            left, right = columns(v)
            xs[f, at : at + 64, 0:256] = left
            xs[f, at : at + 64, 256:512] = v
            xs[f, at : at + 64, 512:768] = right

    def activate(k, f, n, q, v):
        sigma = 0.5 + 0.5 * jnp.tanh(0.5 * v)
        state = v * sigma
        states[k][2**k + f : 2**k + f + n, half(q)] = state.astype(BF).reshape(n, HALF, N)
        slope[k, f : f + n, half(q)] = (sigma + state * (1.0 - sigma)).reshape(n, HALF, N)

    def conv(f, n, q):
        cat = jnp.concatenate(
            [
                xs[f : f + n, 64 * i + HALF * q : 64 * i + HALF * q + HALF, :].reshape(n * HALF, 768)
                for i in range(3)
            ],
            axis=1,
        )
        activate(0, f, n, q, dot(cat, ws[...].reshape(2304, 256)))

    def past(ref, at, n, q):
        return ref[at : at + n, half(q)].reshape(n * HALF, N)

    def temporal(k, f, n, q):
        cat = jnp.concatenate(
            [past(states[k], f + 2**k, n, q), past(states[k], f, n, q)], axis=1
        )
        return dot(cat, wt[k])

    def forward(k, f, n, q):
        activate(k + 1, f, n, q, temporal(k, f, n, q))

    def arrived_state(k, q):
        state_up[q][k].wait()

        @pl.when(t == 0)
        def _():
            states[k][0 : 2**k, half(q)] = jnp.zeros((2**k, HALF, N), BF)
    for q in range(2):
        conv(4, 4, q)
        state_up[q][0].start()
        conv(0, 4, q)
        if q == 0:
            loads[2].wait()
        forward(0, 4, 4, q)
        state_up[q][1].start()
        forward(0, 1, 3, q)
        forward(1, 4, 4, q)
        state_up[q][2].start()
        forward(1, 3, 1, q)
    for i in range(3):
        for j in range(3):
            wsT[i, 256 * j : 256 * j + 256, :] = ws[i, 256 * j : 256 * j + 256, :].T

    @pl.loop(0, 4)
    def _(k):
        wtT[k, 0:256, :] = wt[k, 0:256, :].T
        wtT[k, 256:512, :] = wt[k, 256:512, :].T

    loads[3].wait()

    def back(k, f, n, q):
        source = cot if k == 3 else deltas[k]
        later = past(d3h, f, n, q) if k == 3 else past(deltas[k], f + 2**k, n, q)
        total = dot(jnp.concatenate([past(source, f, n, q), later], axis=1), wtT[k])
        value = (total * past(slope.at[k], f, n, q)).astype(BF)
        target = sd if k == 0 else deltas[k - 1]
        target[f : f + n, half(q)] = value.reshape(n, HALF, N)

    def arrived_delta(k, q):
        delta_dn[q][k].wait()
        at = 0 if k == 3 else 8

        @pl.when(t == 15)
        def _():
            deltas[k][at : at + 2**k, half(q)] = jnp.zeros((2**k, HALF, N), BF)

    for q in range(2):
        arrived_state(0, q)
        forward(0, 0, 1, q)
        arrived_state(1, q)
        forward(1, 0, 3, q)
        forward(2, 4, 4, q)
        arrived_state(2, q)
        forward(2, 0, 4, q)
        state_up[q][3].start()
        arrived_delta(3, q)
        back(3, 0, 4, q)
        delta_dn[q][2].start()
        back(3, 4, 4, q)
        back(2, 0, 4, q)
        delta_dn[q][1].start()
        back(1, 0, 2, q)
        delta_dn[q][0].start()

    def put(ref, tap, value):
        for part in range(16):
            ref[part % 2, part // 2, tap] = value[16 * part : 16 * part + 16].astype(BF)

    def time_grads(k, ref, tap):
        d = 2**k
        for f in range(F):
            src = cot if k == 3 else deltas[k]
            dT[0:256, 256 * f : 256 * f + 256] = src[f].T
            other = d3h[f] if k == 3 else deltas[k][f + d]
            dT[256:512, 256 * f : 256 * f + 256] = other.T
        both = dot(dT[...], states[k][d : d + F].reshape(2048, N))
        put(ref, tap, both[0:256])
        put(ref, tap + 1, both[256:512])

    groups = [
        (g_0, ra_0, ma_0, rb_0),
        (g_1, ra_1, ma_1, rb_1),
        (g_2, ra_2, ma_2, rb_2),
        (g_3, ra_3, ma_3, rb_3),
        (g_x, ra_x, ma_x, rb_x),
        (g_y, ra_y, ma_y, rb_y),
        (g_z, ra_z, ma_z, rb_z),
    ]
    between = [
        remote(g.at[1 - c], ra, a_sem.at[n, 0], a_sem.at[n, 1], (t, sibling))
        for n, (g, ra, _, _) in enumerate(groups)
    ]

    def z_copies(n):
        _, _, ma, rb = groups[n]
        return [
            remote(
                ma.at[lax.rem(z + k, 8)], rb.at[z], b_send.at[n, k], b_recv.at[n, z],
                (t, lax.rem(r + 2 * k, 16)),
            )
            for k in (4, 3, 5, 2, 6, 1, 7)
        ]

    def add_cores(n):
        g, ra, ma, rb = groups[n]
        between[n].wait()

        @pl.loop(0, 8)
        def _(p):
            ma[p] = (g[c, p].astype(F32) + ra[p].astype(F32)).astype(BF)

        for copy in z_copies(n):
            copy.start()
        rb[z] = ma[z]

    def add_z(n, mb, at):
        taps = groups[n][0].shape[2]
        rb = groups[n][3]
        for k in range(1, 8):
            source = lax.rem(z + 8 - k, 8)
            remote(
                rb.at[source], rb.at[source], b_send.at[n, k], b_recv.at[n, source],
                (t, lax.rem(r + 16 - 2 * k, 16)),
            ).wait_recv()
        total = rb[0].astype(F32)
        for p in range(1, 8):
            total = total + rb[p].astype(F32)
        mb[at : at + taps] = total.astype(BF)

    def sent_z(n):
        for copy in z_copies(n):
            copy.wait_send()

    def to_owner(low, high, mb, rc, group, first):
        for k in range(low, high):
            owner = first + k

            @pl.when(t != owner)
            def _():
                remote(
                    mb.at[k], rc.at[t], c_send.at[group, k], c_recv.at[group, t], (owner, r)
                ).start()

    def own_sum(taps, mb, rc, mc, group, first):
        mine = t - first

        @pl.when((t >= first) & (t < first + taps))
        def _():
            rc[t] = mb[mine]
            for k in range(1, 16):
                source = lax.rem(t + k, 16)
                remote(
                    rc.at[source], rc.at[source], c_send.at[group, 0], c_recv.at[group, source],
                    (source, r),
                ).wait_recv()
            total = rc[0].astype(F32)
            for p in range(1, 16):
                total = total + rc[p].astype(F32)
            mc[mine] = total.astype(BF)
            for k in range(1, 16):
                remote(
                    mc.at[mine], mc.at[mine], h_send.at[group, k], h_recv.at[group, mine],
                    (lax.rem(t + k, 16), r),
                ).start()

    def finish(taps, mb, rc, mc, group, first, target):
        mine = t - first
        for k in range(taps):
            owner = first + k

            @pl.when(t != owner)
            def _():
                remote(
                    mb.at[k], rc.at[t], c_send.at[group, k], c_recv.at[group, t], (owner, r)
                ).wait_send()
                remote(
                    mc.at[k], mc.at[k], h_send.at[group, 0], h_recv.at[group, k], (owner, r)
                ).wait_recv()

        target[...] = mc[...].astype(F32) * factor

        @pl.when((t >= first) & (t < first + taps))
        def _():
            for k in range(1, 16):
                remote(
                    mc.at[mine], mc.at[mine], h_send.at[group, k], h_recv.at[group, mine],
                    (lax.rem(t + k, 16), r),
                ).wait_send()
    time_grads(3, g_3, 0)
    between[3].start()
    arrived_delta(2, 0)
    back(2, 4, 4, 0)
    back(1, 2, 2, 0)
    arrived_delta(1, 0)
    back(1, 4, 4, 0)
    back(0, 0, 4, 0)
    add_cores(3)
    arrived_delta(0, 0)
    back(0, 4, 4, 0)
    sd_dn = remote(sd.at[:, 0:64], sd_hi, row_sem.at[6], row_sem.at[7], (t, r_prev))
    sd_dn.start()
    arrived_delta(2, 1)
    back(2, 4, 4, 1)
    back(1, 2, 2, 1)
    time_grads(2, g_2, 0)
    between[2].start()
    arrived_delta(1, 1)
    back(1, 4, 4, 1)
    back(0, 0, 4, 1)
    add_cores(2)
    time_grads(1, g_1, 0)
    between[1].start()
    arrived_delta(0, 1)
    back(0, 4, 4, 1)
    sd_up = remote(sd.at[:, 192:256], sd_lo, row_sem.at[4], row_sem.at[5], (t, r_next))
    sd_up.start()
    add_cores(1)
    time_grads(0, g_0, 0)
    between[0].start()

    def spatial_grads(i, ref):
        rows = xs[:, 64 * i : 64 * i + 256, :].reshape(2048, 768)
        total = dot(dT[0:256, :], rows)
        for j in range(3):
            put(ref, j, total[:, 256 * j : 256 * j + 256])

    for f in range(F):
        dT[0:256, 256 * f : 256 * f + 256] = sd[f].T
    spatial_grads(0, g_x)
    between[4].start()
    spatial_grads(1, g_y)
    between[5].start()
    add_cores(0)
    add_cores(4)
    spatial_grads(2, g_z)
    between[6].start()
    add_cores(5)

    @pl.loop(0, F)
    def _(f):
        v = sd[f]
        left, right = columns(v)
        ys[f, 64:320, 0:256] = right
        ys[f, 64:320, 256:512] = v
        ys[f, 64:320, 512:768] = left

    add_cores(6)
    sd_up.wait()
    sd_dn.wait()

    @pl.when(r == 0)
    def _():
        sd_lo[...] = jnp.zeros_like(sd_lo)

    @pl.when(r == 15)
    def _():
        sd_hi[...] = jnp.zeros_like(sd_hi)

    @pl.loop(0, F)
    def _(f):
        for ref, at in ((sd_lo, 0), (sd_hi, 320)):
            v = ref[f]
            left, right = columns(v)
            ys[f, at : at + 64, 0:256] = right
            ys[f, at : at + 64, 256:512] = v
            ys[f, at : at + 64, 512:768] = left
    def input_grads(f, n, q):
        cat = jnp.concatenate(
            [
                ys[f : f + n, 64 * (2 - i) + HALF * q : 64 * (2 - i) + HALF * q + HALF, :].reshape(
                    n * HALF, 768
                )
                for i in range(3)
            ],
            axis=1,
        )
        total = dot(cat, wsT[...].reshape(2304, 256)) + past(cot, f, n, q).astype(F32)
        gin[f : f + n, half(q)] = total.astype(BF).reshape(n, HALF, N)

    def outputs(f, n, q):
        total = temporal(3, f, n, q) + past(lat, f, n, q).astype(F32)
        out[f : f + n, half(q)] = total.astype(BF).reshape(n, HALF, N)

    input_grads(0, 4, 0)
    input_grads(4, 4, 0)
    input_grads(0, 4, 1)
    input_grads(4, 4, 1)
    for k in (3, 2, 1, 0):
        add_z(k, mb_t, 2 * k)
        to_owner(2 * k, 2 * k + 2, mb_t, rc_t, 0, 8)
    arrived_state(3, 0)
    outputs(0, 4, 0)
    outputs(4, 4, 0)
    add_z(4, mb_s, 0)
    to_owner(0, 3, mb_s, rc_s, 1, 0)
    own_sum(8, mb_t, rc_t, mc_t, 0, 8)
    arrived_state(3, 1)
    outputs(0, 4, 1)
    outputs(4, 4, 1)
    add_z(5, mb_s, 3)
    to_owner(3, 6, mb_s, rc_s, 1, 0)
    add_z(6, mb_s, 6)
    to_owner(6, 9, mb_s, rc_s, 1, 0)
    own_sum(9, mb_s, rc_s, mc_s, 1, 0)
    for n in range(7):
        sent_z(n)
    finish(8, mb_t, rc_t, mc_t, 0, 8, gt_out)
    finish(9, mb_s, rc_s, mc_s, 1, 0, gs_out)
def handed_on(*refs):
    sem = refs[-1]
    parts = [(k, slice(4 * p, 4 * p + 4)) for k in (0, 1) for p in range(2)]
    parts += [(2, slice(0, 9)), (3, slice(0, 8))]
    stores = [
        pltpu.make_async_copy(refs[k].at[at], refs[4 + k].at[at], sem.at[n])
        for n, (k, at) in enumerate(parts)
    ]
    for copy in stores:
        copy.start()
    for copy in stores:
        copy.wait()


def shards(latents, cotangent, w_spatial, w_time):
    shape = latents.shape
    vmem = pl.BlockSpec(memory_space=pltpu.VMEM)
    hbm = pl.BlockSpec(memory_space=pl.ANY)
    V = pltpu.VMEM
    DMA = pltpu.SemaphoreType.DMA
    sizes = (2, 2, 2, 2, 3, 3, 3)
    scratch = [
        V((F, N, N), BF), V((F, N, N), BF), V((3, 768, N), BF), V((4, 512, N), BF),
        V((F, 384, 768), BF), V((F, 384, 768), BF),
        V((F, 64, N), BF), V((F, 64, N), BF), V((F, 64, N), BF), V((F, 64, N), BF),
        V((9, N, N), BF), V((10, N, N), BF), V((12, N, N), BF), V((16, N, N), BF),
        V((4, F, N, N), F32),
        V((9, N, N), BF), V((10, N, N), BF), V((12, N, N), BF), V((F, N, N), BF), V((F, N, N), BF),
        V((512, 2048), BF), V((3, 768, 256), BF), V((4, 512, 256), BF),
        *[V((2, 8, n, 16, N), BF) for n in sizes],
        *[V((8, n, 16, N), BF) for n in sizes],
        *[V((8, n, 16, N), BF) for n in sizes],
        *[V((8, n, 16, N), BF) for n in sizes],
        V((8, 16, N), BF), V((9, 16, N), BF),
        V((16, 16, N), BF), V((16, 16, N), BF),
        V((8, 16, N), BF), V((9, 16, N), BF),
        DMA((4,)), DMA((8,)), DMA((2, 8)), DMA((2, 8)), DMA((7, 2)),
        DMA((7, 8)), DMA((7, 8)), DMA((2, 9)), DMA((2, 16)), DMA((2, 16)), DMA((2, 9)),
    ]
    results = [
        jax.ShapeDtypeStruct((F, N, N), BF),
        jax.ShapeDtypeStruct((F, N, N), BF),
        jax.ShapeDtypeStruct((9, 16, N), F32),
        jax.ShapeDtypeStruct((8, 16, N), F32),
    ]
    held = pl.pallas_call(
        kernel,
        out_shape=[V(x.shape, x.dtype) for x in results],
        in_specs=[hbm] * 4,
        out_specs=[vmem] * 4,
        scratch_shapes=scratch,
        compiler_params=pltpu.CompilerParams(
            collective_id=0, has_side_effects=True, vmem_limit_bytes=57 * 1024 * 1024
        ),
        cost_estimate=pl.CostEstimate(
            flops=51 * 2 * 2048 * N * N, bytes_accessed=7 * 1024 * 1024, transcendentals=4 * 2048 * N
        ),
    )(
        latents.reshape(F, N, N), cotangent.reshape(F, N, N),
        w_spatial.reshape(3, 768, N), w_time.reshape(4, 512, N),
    )
    out, gin, gs, gt = pl.pallas_call(
        handed_on,
        out_shape=results,
        in_specs=[vmem] * 4,
        out_specs=[hbm] * 4,
        scratch_shapes=[DMA((6,))],
        cost_estimate=pl.CostEstimate(flops=0, bytes_accessed=5 * 1024 * 1024, transcendentals=0),
    )(*[pltpu.with_memory_space_constraint(x, V) for x in held])
    spatial = jnp.swapaxes(gs, 1, 2)
    time = jnp.swapaxes(gt, 1, 2).reshape(4, 2, N, 16)
    return out.reshape(shape), gin.reshape(shape), spatial, time


def solution(mesh):
    in_specs = (P("tm", "rows", None, None), P("tm", "rows", None, None), P(), P())
    out_specs = (
        P("tm", "rows", None, None),
        P("tm", "rows", None, None),
        P(None, None, "rows"),
        P(None, None, None, "rows"),
    )
    return jax.shard_map(shards, mesh=mesh, in_specs=in_specs, out_specs=out_specs, check_vma=False)
```
